32 devices in a mesh: orb: 16 (over z, y, core), slab: 2 (over x).
Axes of the slice: x: 2, y: 2, z: 4, core: 2. Of those that a mesh axis runs over, the one named last changes fastest.
Arguments:
- orbitals: bfloat16 [16, 64, 4096], P('orb', 'slab'), may hold values from -6 to 6
- partners: int32 [16, 2], P('orb'), may hold values from 0 to 15, as said below
- offsets: int32 [16, 3], P('orb'), may hold values from 0 to 32
- kernel: float32 [128, 128, 128], P(None, 'slab'), may hold values from 0.5 to 8
Outputs:
- exchange: float32 [16, 64, 4096], P('orb', 'slab')
The draws below stay inside these ranges and needn't reach their ends.
Inputs may be any that keep to these rules, and one draw needn't show every extreme that they name: Orbital i's two partners differ from each other and equal (i + e) mod 16 with 1 <= e <= 4.
All inputs are finite; a program needn't handle non-finite values.
Results may differ from the reference program's by a relative error of at most 0.0042.
Values may be sent and summed in bfloat16 or wider, within the bound.
A program may use at most 128 MiB of HBM per device.

```python
import math
import jax
import jax.numpy as jnp
from jax import lax

B = 64
G = 128
ORB_DEV = 1
REACH = 4
ORBITALS = 16


def draw_partners(key, part):
    reach_orbits = REACH * ORB_DEV
    first_key, second_key = jax.random.split(key)
    nearer = jax.random.randint(first_key, (ORBITALS,), 1, reach_orbits + 1)
    second_step = jax.random.randint(second_key, (ORBITALS,), 1, reach_orbits)
    farther = (nearer - 1 + second_step) % reach_orbits + 1
    orbit_ids = jnp.arange(ORBITALS, dtype=jnp.int32)
    return jnp.stack([(orbit_ids + nearer) % ORBITALS, (orbit_ids + farther) % ORBITALS], axis=1).astype(jnp.int32)


def touch_ends(drawn, own_key, smallest, largest):
    extent = drawn.shape
    place = [jax.random.randint(jax.random.fold_in(own_key, axis), (), 0, extent[axis]) for axis in range(len(extent))]
    drawn = drawn.at[tuple(place)].set(smallest)
    longest = extent.index(max(extent))
    place[longest] = (place[longest] + 1) % extent[longest]
    return drawn.at[tuple(place)].set(largest)


def block_levels(own_key, shape, pieces, low, top_value):
    def one(position, parts):
        heights = jax.random.uniform(jax.random.fold_in(jax.random.fold_in(own_key, 6), position), (parts,), jnp.float32, low / len(pieces), top_value / len(pieces))
        return jnp.repeat(jnp.exp(heights), shape[position] // parts).reshape((-1,) + (1,) * (len(shape) - position - 1))

    loudness = one(*pieces[0])
    for cut in pieces[1:]:
        loudness = loudness * one(*cut)
    return loudness


def bell_draw(stream_key, shape, width, bound, pieces=(), held_as=jnp.bfloat16):
    gain = block_levels(stream_key, shape, pieces, -0.22, 0.18) if pieces else 1.0
    values = jax.random.normal(stream_key, shape, jnp.float32) * width * gain
    return jnp.minimum(jnp.maximum(values, -bound), bound).astype(held_as)


def setup_inputs(seed: int = 0) -> dict:
    seeds = jax.random.split(jax.random.key(seed), 5)
    orbitals = bell_draw(seeds[0], (ORBITALS, B, B * B), 1.0, 6.0, ((0, 16), (1, 2)))
    partners = draw_partners(jax.random.fold_in(seeds[4], 71), 0)
    offsets = touch_ends(jax.random.randint(seeds[2], (ORBITALS, 3), 0, B // 2 + 1), jax.random.fold_in(seeds[2], 1), 0, (B // 2 + 1) - 1).astype(jnp.int32)
    kernel = jnp.clip(jnp.exp(math.log(8.0) - 2.7725887 * jax.random.uniform(seeds[3], (G, G, G), jnp.float32) ** block_levels(seeds[3], (G, G, G), ((1, 2),), -0.2, 0.2)), 0.5, 8.0)
    return {"orbitals": orbitals, "partners": partners, "offsets": offsets, "kernel": kernel}


def phase_table(length, offset, grid_len, signed):
    frequency = jnp.arange(grid_len, dtype=jnp.int32)
    places = offset + jnp.arange(length, dtype=jnp.int32)
    wrapped = (places[:, None] * frequency[None, :]) % grid_len
    angles = wrapped.astype(jnp.float32) * (2.0 * math.pi / grid_len)
    return jnp.cos(angles).astype(jnp.bfloat16), (signed * jnp.sin(angles)).astype(jnp.bfloat16)


def move_box(orbital_box, displacement, row_start, row_count):
    half_edge = orbital_box.shape[0] // 2
    padded = jnp.pad(orbital_box, half_edge)
    starts = (row_start + half_edge + displacement[0], half_edge + displacement[1], half_edge + displacement[2])
    return lax.dynamic_slice(padded, starts, (row_count, orbital_box.shape[1], orbital_box.shape[2]))


def mixed(form, left_side, right_side):
    return jnp.einsum(form, left_side.astype(jnp.float32), right_side.astype(jnp.float32))


def complex_pair(form, cos_table, sin_table, real_part, imag_part):
    real_out = mixed(form, cos_table, real_part) - mixed(form, sin_table, imag_part)
    imag_out = mixed(form, cos_table, imag_part) + mixed(form, sin_table, real_part)
    return real_out, imag_out


def box_tables(box_edge, half_edge, grid_len, displace_part):
    own_cos, own_sin = phase_table(box_edge, half_edge, grid_len, 1.0)
    far_cos, far_sin = phase_table(box_edge, half_edge + displace_part, grid_len, 1.0)
    return jnp.stack([own_cos, far_cos], 0), jnp.stack([own_sin, far_sin], 0)


def pair_terms(own_box, partner_box, displace, kernel):
    box_edge = own_box.shape[0]
    grid_len = 2 * box_edge
    half_edge = box_edge // 2
    partner_here = move_box(partner_box, -displace, 0, box_edge)
    own_there = move_box(own_box, displace, 0, box_edge)
    density = (own_box.astype(jnp.float32) * partner_here.astype(jnp.float32)).astype(jnp.bfloat16)
    fwd_cos, fwd_sin = phase_table(box_edge, half_edge, grid_len, -1.0)
    z_real = mixed('ayz,zk->ayk', density, fwd_cos).astype(jnp.bfloat16)
    z_imag = mixed('ayz,zk->ayk', density, fwd_sin).astype(jnp.bfloat16)
    y_real, y_imag = complex_pair('yk,ayq->akq', fwd_cos, fwd_sin, z_real, z_imag)
    y_real, y_imag = y_real.astype(jnp.bfloat16), y_imag.astype(jnp.bfloat16)
    x_real, x_imag = complex_pair('ak,aqz->kqz', fwd_cos, fwd_sin, y_real, y_imag)
    w_real = (kernel * x_real).astype(jnp.bfloat16)
    w_imag = (kernel * x_imag).astype(jnp.bfloat16)
    row_cos, row_sin = box_tables(box_edge, half_edge, grid_len, displace[0])
    v_real, v_imag = complex_pair('mak,kqz->maqz', row_cos, row_sin, w_real, w_imag)
    v_real, v_imag = v_real.astype(jnp.bfloat16), v_imag.astype(jnp.bfloat16)
    col_cos, col_sin = box_tables(box_edge, half_edge, grid_len, displace[1])
    u_real, u_imag = complex_pair('myk,makz->mayz', col_cos, col_sin, v_real, v_imag)
    u_real, u_imag = u_real.astype(jnp.bfloat16), u_imag.astype(jnp.bfloat16)
    dep_cos, dep_sin = box_tables(box_edge, half_edge, grid_len, displace[2])
    field = (mixed('mzk,mayk->mayz', dep_cos, u_real) - mixed('mzk,mayk->mayz', dep_sin, u_imag)) * (1.0 / grid_len ** 3)
    own_term = field[0] * partner_here.astype(jnp.float32)
    far_term = field[1] * own_there.astype(jnp.float32)
    return own_term, far_term


def reference(orbitals, partners, offsets, kernel):
    orbit_count = orbitals.shape[0]
    box_edge = orbitals.shape[1]
    boxes = orbitals.reshape(orbit_count, box_edge, box_edge, box_edge)
    partner_list = partners.reshape(-1)

    def visit(total_field, pair_index):
        own_index = pair_index // 2
        partner_index = partner_list[pair_index]
        displace = offsets[partner_index] - offsets[own_index]
        own_term, far_term = pair_terms(boxes[own_index], boxes[partner_index], displace, kernel)
        total_field = total_field.at[own_index].add(own_term).at[partner_index].add(far_term)
        return total_field, None

    empty_field = jnp.zeros((orbit_count, box_edge, box_edge, box_edge), jnp.float32)
    total_field, unused_out = lax.scan(visit, empty_field, jnp.arange(partner_list.shape[0], dtype=jnp.int32))
    return total_field.reshape(orbit_count, box_edge, box_edge * box_edge)
```

```python
import functools
import math

import jax
import jax.numpy as jnp
import ml_dtypes
import numpy as np
from jax import lax
from jax.experimental import pallas as pl
from jax.experimental.pallas import tpu as pltpu
from jax.sharding import PartitionSpec as P

REACH = 4
F32 = jnp.float32
BF16 = jnp.bfloat16


def passed_along(block, axis, distance):
    devices = range(lax.axis_size(axis))
    route = [((i - distance) % len(devices), i) for i in devices]
    return lax.ppermute(block, axis, route)


def phases(places, frequency, grid_len, signed):
    wrapped = (places[:, None] * frequency[None, :]) % grid_len
    angles = wrapped.astype(np.float64) * (2.0 * math.pi / grid_len)
    return np.cos(angles), signed * np.sin(angles)


def block_form(cos, sin):
    return np.block([[cos, -sin], [sin, cos]])


def make_tables(box_edge, slab_count):
    grid_len = 2 * box_edge
    half = box_edge // 2
    k1_count = grid_len // slab_count
    box = np.arange(box_edge) + half
    grid = np.arange(grid_len)
    cos, sin = phases(box, grid, grid_len, -1.0)
    f2 = np.zeros((2 * box_edge, 2 * grid_len))
    f2[:box_edge] = np.concatenate([cos, sin], 1)
    f0 = block_form(cos.T, sin.T)
    f1 = []
    e1 = []
    gcos, gsin = phases(grid, grid, grid_len, 1.0)
    for s in range(slab_count):
        mine = slice(s * k1_count, (s + 1) * k1_count)
        f1.append(block_form(cos.T[mine], sin.T[mine]))
        e1.append(block_form(gcos[:, mine], gsin[:, mine]))
    e0 = block_form(gcos, gsin)
    e2 = np.concatenate([gcos.T, -gsin.T], 0) / grid_len**3
    tables = [f2, np.stack(f1), f0, e0, np.stack(e1), e2]
    return [t.astype(np.float32).astype(ml_dtypes.bfloat16) for t in tables]


def dot(a, b):
    return jnp.dot(a, b, preferred_element_type=F32)


def pair_kernel(
    box_edge, k1_count,
    shift_ref, slab_ref,
    boxes_ref, kernel_ref, f2_ref, f1_ref, f0_ref, e0_ref, e1_ref, e2_ref,
    out_ref,
    cells, here, y_parts, v_parts, terms, e1_own, e1_far, e2_own, e2_far,
):
    edge = box_edge
    grid_len = 2 * edge
    half = edge // 2
    lanes = 2 * edge
    slab = slab_ref[0]
    lane = lax.broadcasted_iota(jnp.int32, (edge, lanes), 1)
    low_lanes = lane < edge
    row = lax.broadcasted_iota(jnp.int32, (edge, lanes), 0)
    shifts = [[shift_ref[n, c] for c in range(3)] for n in range(2)]

    e1_grid = e1_ref[slab]
    e2_grid = e2_ref[...]
    sel_lane = lax.broadcasted_iota(jnp.int32, (grid_len, lanes), 1)
    sel_row = lax.broadcasted_iota(jnp.int32, (grid_len, lanes), 0)

    def windows(d1, d2):
        pick_rows = (row + half + d1 == lane).astype(F32).astype(BF16)
        top = dot(pick_rows, e1_grid[:grid_len]).astype(BF16)
        bottom = dot(pick_rows, e1_grid[grid_len:]).astype(BF16)
        pick_cols = ((sel_lane + half + d2 == sel_row) & (sel_lane < edge)).astype(F32).astype(BF16)
        return jnp.concatenate([top, bottom], 0), dot(e2_grid, pick_cols).astype(BF16)

    e1_own[...], e2_own[...] = windows(0, 0)
    for n in range(2):
        e1_far[n], e2_far[n] = windows(shifts[n][1], shifts[n][2])

    def unpack(g, carry):
        lo_at = pl.ds(2 * g, edge, stride=edge)
        hi_at = pl.ds(2 * g + 1, edge, stride=edge)
        for b in range(3):
            both = boxes_ref[b, :, pl.ds(pl.multiple_of(g * lanes, lanes), lanes)].astype(F32)
            cells[b, lo_at, :] = jnp.where(low_lanes, both, 0.0)
            cells[b, hi_at, :] = jnp.where(low_lanes, pltpu.roll(both, edge, 1), 0.0)
        return carry

    lax.fori_loop(0, edge // 2, unpack, 0, unroll=2)

    def moved(b, c0, d0, d1, d2):
        source = c0 + d0
        at = jnp.clip(source, 0, edge - 1)
        block = cells[b, pl.ds(pl.multiple_of(at * edge, edge), edge), :]
        block = pltpu.roll(block, (-d2) & (lanes - 1), 1)
        block = pltpu.roll(block, (-d1) & (edge - 1), 0)
        inside = (row + d1 >= 0) & (row + d1 < edge) & (source >= 0) & (source < edge)
        return jnp.where(inside, block, 0.0)

    def forward(c0, carry):
        at = pl.ds(pl.multiple_of(c0 * edge, edge), edge)
        own = cells[0, at, :]
        z = []
        for n in range(2):
            d0, d1, d2 = shifts[n]
            partner = moved(1 + n, c0, -d0, -d1, -d2)
            here[n, at, :] = partner
            z.append((own * partner).astype(BF16))
        z = dot(jnp.concatenate(z, 0), f2_ref[...]).astype(BF16)
        z = jnp.concatenate(
            [
                jnp.concatenate([z[n * edge : (n + 1) * edge, :grid_len], z[n * edge : (n + 1) * edge, grid_len:]], 0)
                for n in range(2)
            ],
            1,
        )
        y = dot(f1_ref[slab], z)
        for n in range(2):
            part = y[:, n * grid_len : (n + 1) * grid_len]
            y_parts[n, pl.ds(c0, k1_count, stride=2 * edge), :] = part[:k1_count]
            y_parts[n, pl.ds(edge + c0, k1_count, stride=2 * edge), :] = part[k1_count:]
        return carry

    lax.fori_loop(0, edge, forward, 0, unroll=4)

    def middle(k1, carry):
        at = pl.ds(pl.multiple_of(k1 * 2 * edge, 2 * edge), 2 * edge)
        y = jnp.concatenate([y_parts[n, at, :].astype(BF16) for n in range(2)], 1)
        x = dot(f0_ref[...], y)
        k = kernel_ref[pl.ds(k1, grid_len, stride=k1_count), :]
        k = jnp.concatenate([k, k], 1)
        w = jnp.concatenate([(x[:grid_len] * k).astype(BF16), (x[grid_len:] * k).astype(BF16)], 0)
        v = dot(e0_ref[...], w)
        for n in range(2):
            part = v[:, n * grid_len : (n + 1) * grid_len]
            v_parts[n, pl.ds(k1, grid_len, stride=2 * k1_count), :] = part[:grid_len]
            v_parts[n, pl.ds(k1_count + k1, grid_len, stride=2 * k1_count), :] = part[grid_len:]
        return carry

    lax.fori_loop(0, k1_count, middle, 0, unroll=4)

    def v_rows(n, u0):
        at = pl.ds(pl.multiple_of(u0 * 2 * k1_count, 2 * k1_count), 2 * k1_count)
        return v_parts[n, at, :].astype(BF16)

    def backward(c0, carry):
        at = pl.ds(pl.multiple_of(c0 * edge, edge), edge)
        v = jnp.concatenate([v_rows(n, half + c0) for n in range(2)], 1)
        u = dot(e1_own[...], v).astype(BF16)
        u = jnp.concatenate(
            [
                jnp.concatenate([u[:edge, n * grid_len : (n + 1) * grid_len], u[edge:, n * grid_len : (n + 1) * grid_len]], 1)
                for n in range(2)
            ],
            0,
        )
        field = dot(u, e2_own[...])
        terms[0, at, :] = field[:edge] * here[0, at, :] + field[edge:] * here[1, at, :]
        for n in range(2):
            d0, d1, d2 = shifts[n]
            u = dot(e1_far[n], v_rows(n, half + d0 + c0)).astype(BF16)
            field = dot(jnp.concatenate([u[:edge], u[edge:]], 1), e2_far[n])
            terms[1 + n, at, :] = field * moved(0, c0, d0, d1, d2)
        return carry

    lax.fori_loop(0, edge, backward, 0, unroll=4)

    def pack(g, carry):
        for b in range(3):
            lo = terms[b, pl.ds(2 * g, edge, stride=edge), :]
            hi = terms[b, pl.ds(2 * g + 1, edge, stride=edge), :]
            both = lo + pltpu.roll(hi, edge, 1)
            out_ref[b, :, pl.ds(pl.multiple_of(g * lanes, lanes), lanes)] = both.astype(BF16)
        return carry

    lax.fori_loop(0, edge // 2, pack, 0, unroll=2)


def pair_terms(boxes, displace, slab_index, kernel, slab_count):
    box_edge = boxes.shape[1]
    grid_len, k1_count = kernel.shape[0], kernel.shape[1]
    tables = make_tables(box_edge, slab_count)
    smem = pl.BlockSpec(memory_space=pltpu.SMEM)
    vmem = pl.BlockSpec(memory_space=pltpu.VMEM)
    cells = box_edge * box_edge
    lanes = 2 * box_edge
    return pl.pallas_call(
        functools.partial(pair_kernel, box_edge, k1_count),
        out_shape=jax.ShapeDtypeStruct(boxes.shape, BF16),
        in_specs=[smem, smem] + [vmem] * 8,
        out_specs=vmem,
        scratch_shapes=[
            pltpu.VMEM((3, cells, lanes), F32),
            pltpu.VMEM((2, cells, lanes), F32),
            pltpu.VMEM((2, k1_count * 2 * box_edge, grid_len), F32),
            pltpu.VMEM((2, grid_len * 2 * k1_count, grid_len), F32),
            pltpu.VMEM((3, cells, lanes), F32),
            pltpu.VMEM((2 * box_edge, 2 * k1_count), BF16),
            pltpu.VMEM((2, 2 * box_edge, 2 * k1_count), BF16),
            pltpu.VMEM((2 * grid_len, lanes), BF16),
            pltpu.VMEM((2, 2 * grid_len, lanes), BF16),
        ],
        compiler_params=pltpu.CompilerParams(vmem_limit_bytes=60 * 1024 * 1024),
        name="pair_terms",
    )(displace, slab_index, boxes, kernel.reshape(grid_len * k1_count, grid_len), *tables)


def per_device(orbitals, partners, offsets, kernel):
    slab_count = lax.axis_size("slab")
    spread = lax.axis_size("orb")
    orbit_index = lax.axis_index("orb")
    slab_index = lax.axis_index("slab")
    slab_rows = orbitals.shape[1]

    corners = lax.all_gather(offsets, "orb", axis=0, tiled=True)
    held = [orbitals] + [passed_along(orbitals, "orb", -hop) for hop in range(1, REACH + 1)]
    held = jnp.concatenate(held, 0)
    partner_ids = partners.reshape(2)
    hop_of_pair = (partner_ids - orbit_index) % spread
    displace = corners[partner_ids] - offsets
    sent = jnp.concatenate([orbitals, held[hop_of_pair]], 0)
    boxes = lax.all_gather(sent, "slab", axis=1, tiled=True)

    terms = pair_terms(boxes, displace, slab_index[None], kernel, slab_count)

    terms = terms.reshape(3, slab_count, slab_rows, terms.shape[2])
    arrived = lax.all_to_all(terms, "slab", split_axis=1, concat_axis=1, tiled=True)
    total = arrived.astype(F32).sum(1)
    result = total[0]
    far = total[1:].astype(BF16)
    for hop in range(1, REACH + 1):
        bucket = jnp.where(hop_of_pair[0] == hop, far[0], jnp.where(hop_of_pair[1] == hop, far[1], jnp.zeros_like(far[0])))
        result = result + passed_along(bucket, "orb", hop).astype(F32)
    return result[None]


def solution(mesh):
    return jax.shard_map(
        per_device,
        mesh=mesh,
        in_specs=(P("orb", "slab", None), P("orb", None), P("orb", None), P(None, "slab", None)),
        out_specs=P("orb", "slab", None),
        check_vma=False,
    )
```

```python
import functools
import math

import jax
import jax.numpy as jnp
import ml_dtypes
import numpy as np
from jax import lax
from jax.experimental import pallas as pl
from jax.experimental.pallas import tpu as pltpu
from jax.sharding import PartitionSpec as P

REACH = 4
F32 = jnp.float32
BF16 = jnp.bfloat16


def phases(places, frequency, grid_len, signed):
    wrapped = (places[:, None] * frequency[None, :]) % grid_len
    angles = wrapped.astype(np.float64) * (2.0 * math.pi / grid_len)
    return np.cos(angles), signed * np.sin(angles)


def block_form(cos, sin):
    return np.block([[cos, -sin], [sin, cos]])


def make_tables(box_edge, slab_count):
    grid_len = 2 * box_edge
    half = box_edge // 2
    k1_count = grid_len // slab_count
    box = np.arange(box_edge) + half
    grid = np.arange(grid_len)
    cos, sin = phases(box, grid, grid_len, -1.0)
    f2 = np.zeros((2 * box_edge, 2 * grid_len))
    f2[:box_edge] = np.concatenate([cos, sin], 1)
    f0 = block_form(cos.T, sin.T)
    f1 = []
    e1 = []
    gcos, gsin = phases(grid, grid, grid_len, 1.0)
    for s in range(slab_count):
        mine = slice(s * k1_count, (s + 1) * k1_count)
        f1.append(block_form(cos.T[mine], sin.T[mine]))
        e1.append(block_form(gcos[:, mine], gsin[:, mine]))
    e0 = block_form(gcos, gsin)
    e2 = np.concatenate([gcos.T, -gsin.T], 0) / grid_len**3
    tables = [f2, np.stack(f1), f0, e0, np.stack(e1), e2]
    return [t.astype(np.float32).astype(ml_dtypes.bfloat16) for t in tables]


def dot(a, b):
    return jnp.dot(a, b, preferred_element_type=F32)


def pair_kernel(
    box_edge, k1_count,
    slab_ref,
    boxes_ref, kernel_ref, f2_ref, f1_ref, f0_ref, e0_ref, e1_ref, e2_ref,
    out_ref,
    cells, here, y_parts, v_parts, terms, e1_own, e1_far, e2_own, e2_far,
):
    edge = box_edge
    grid_len = 2 * edge
    half = edge // 2
    lanes = 2 * edge
    slab_count = boxes_ref.shape[0]
    slab = slab_ref[0]
    lane = lax.broadcasted_iota(jnp.int32, (edge, lanes), 1)
    low_lanes = lane < edge
    row = lax.broadcasted_iota(jnp.int32, (edge, lanes), 0)
    corner_lane = lax.broadcasted_iota(jnp.int32, (1, lanes), 1)

    def corner(b):
        held = boxes_ref[0, b, :, pl.ds(edge * edge, lanes)].astype(F32)[0:1]
        return [jnp.sum(jnp.where(corner_lane == c, held, 0.0)).astype(jnp.int32) for c in range(3)]

    corners = [corner(b) for b in range(3)]
    shifts = [[corners[1 + n][c] - corners[0][c] for c in range(3)] for n in range(2)]
    cell_pitch = edge + 1
    y_pitch = 2 * edge + 1
    v_pitch = 2 * k1_count + 1

    e1_grid = e1_ref[slab]
    e2_grid = e2_ref[...]
    sel_lane = lax.broadcasted_iota(jnp.int32, (grid_len, lanes), 1)
    sel_row = lax.broadcasted_iota(jnp.int32, (grid_len, lanes), 0)

    def windows(d1, d2):
        pick_rows = (row + half + d1 == lane).astype(F32).astype(BF16)
        top = dot(pick_rows, e1_grid[:grid_len]).astype(BF16)
        bottom = dot(pick_rows, e1_grid[grid_len:]).astype(BF16)
        pick_cols = ((sel_lane + half + d2 == sel_row) & (sel_lane < edge)).astype(F32).astype(BF16)
        return jnp.concatenate([top, bottom], 0), dot(e2_grid, pick_cols).astype(BF16)

    e1_own[...], e2_own[...] = windows(0, 0)
    for n in range(2):
        e1_far[n], e2_far[n] = windows(shifts[n][1], shifts[n][2])

    def unpack(g, carry):
        lo_at = pl.ds(2 * g, edge, stride=cell_pitch)
        hi_at = pl.ds(2 * g + 1, edge, stride=cell_pitch)
        for b in range(3):
            both = boxes_ref[:, b, :, pl.ds(pl.multiple_of(g * lanes, lanes), lanes)].astype(F32)
            both = both.reshape(edge, lanes)
            cells[b, lo_at, :] = jnp.where(low_lanes, both, 0.0)
            cells[b, hi_at, :] = jnp.where(low_lanes, pltpu.roll(both, edge, 1), 0.0)
        return carry

    lax.fori_loop(0, edge // 2, unpack, 0, unroll=2)

    def moved(b, c0, d0, d1, d2):
        source = c0 + d0
        at = jnp.clip(source, 0, edge - 1)
        block = cells[b, pl.ds(at * cell_pitch, edge), :]
        block = pltpu.roll(block, (-d2) & (lanes - 1), 1)
        block = pltpu.roll(block, (-d1) & (edge - 1), 0)
        inside = (row + d1 >= 0) & (row + d1 < edge) & (source >= 0) & (source < edge)
        return jnp.where(inside, block, 0.0)

    def forward(c0, carry):
        at = pl.ds(pl.multiple_of(c0 * edge, edge), edge)
        own = cells[0, pl.ds(c0 * cell_pitch, edge), :]
        z = []
        for n in range(2):
            d0, d1, d2 = shifts[n]
            partner = moved(1 + n, c0, -d0, -d1, -d2)
            here[n, at, :] = partner
            z.append((own * partner).astype(BF16))
        z = dot(jnp.concatenate(z, 0), f2_ref[...]).astype(BF16)
        z = jnp.concatenate(
            [
                jnp.concatenate([z[n * edge : (n + 1) * edge, :grid_len], z[n * edge : (n + 1) * edge, grid_len:]], 0)
                for n in range(2)
            ],
            1,
        )
        y = dot(f1_ref[slab], z)
        for n in range(2):
            part = y[:, n * grid_len : (n + 1) * grid_len]
            y_parts[n, pl.ds(c0, k1_count, stride=y_pitch), :] = part[:k1_count]
            y_parts[n, pl.ds(edge + c0, k1_count, stride=y_pitch), :] = part[k1_count:]
        return carry

    lax.fori_loop(0, edge, forward, 0, unroll=4)

    def middle(k1, carry):
        at = pl.ds(k1 * y_pitch, 2 * edge)
        y = jnp.concatenate([y_parts[n, at, :].astype(BF16) for n in range(2)], 1)
        x = dot(f0_ref[...], y)
        k = kernel_ref[pl.ds(k1, grid_len, stride=k1_count), :]
        k = jnp.concatenate([k, k], 1)
        w = jnp.concatenate([(x[:grid_len] * k).astype(BF16), (x[grid_len:] * k).astype(BF16)], 0)
        v = dot(e0_ref[...], w)
        for n in range(2):
            part = v[:, n * grid_len : (n + 1) * grid_len]
            v_parts[n, pl.ds(k1, grid_len, stride=v_pitch), :] = part[:grid_len]
            v_parts[n, pl.ds(k1_count + k1, grid_len, stride=v_pitch), :] = part[grid_len:]
        return carry

    lax.fori_loop(0, k1_count, middle, 0, unroll=4)

    def v_rows(n, u0):
        at = pl.ds(u0 * v_pitch, 2 * k1_count)
        return v_parts[n, at, :].astype(BF16)

    def backward(c0, carry):
        at = pl.ds(pl.multiple_of(c0 * edge, edge), edge)
        v = jnp.concatenate([v_rows(n, half + c0) for n in range(2)], 1)
        u = dot(e1_own[...], v).astype(BF16)
        u = jnp.concatenate(
            [
                jnp.concatenate([u[:edge, n * grid_len : (n + 1) * grid_len], u[edge:, n * grid_len : (n + 1) * grid_len]], 1)
                for n in range(2)
            ],
            0,
        )
        field = dot(u, e2_own[...])
        to = pl.ds(c0 * cell_pitch, edge)
        terms[0, to, :] = field[:edge] * here[0, at, :] + field[edge:] * here[1, at, :]
        for n in range(2):
            d0, d1, d2 = shifts[n]
            u = dot(e1_far[n], v_rows(n, half + d0 + c0)).astype(BF16)
            field = dot(jnp.concatenate([u[:edge], u[edge:]], 1), e2_far[n])
            terms[1 + n, to, :] = field * moved(0, c0, d0, d1, d2)
        return carry

    lax.fori_loop(0, edge, backward, 0, unroll=4)

    def pack(g, carry):
        for b in range(3):
            lo = terms[b, pl.ds(2 * g, edge, stride=cell_pitch), :]
            hi = terms[b, pl.ds(2 * g + 1, edge, stride=cell_pitch), :]
            both = (lo + pltpu.roll(hi, edge, 1)).reshape(slab_count, edge // slab_count, lanes)
            out_ref[:, b, :, pl.ds(pl.multiple_of(g * lanes, lanes), lanes)] = both.astype(BF16)
        return carry

    lax.fori_loop(0, edge // 2, pack, 0, unroll=2)


def pair_terms(boxes, slab_index, kernel):
    slab_count, _, rows, _ = boxes.shape
    box_edge = slab_count * rows
    grid_len, k1_count = kernel.shape[0], kernel.shape[1]
    tables = make_tables(box_edge, slab_count)
    smem = pl.BlockSpec(memory_space=pltpu.SMEM)
    vmem = pl.BlockSpec(memory_space=pltpu.VMEM)
    cells = box_edge * box_edge
    cell_rows = box_edge * (box_edge + 1)
    lanes = 2 * box_edge
    return pl.pallas_call(
        functools.partial(pair_kernel, box_edge, k1_count),
        out_shape=jax.ShapeDtypeStruct((slab_count, 3, rows, cells), BF16),
        in_specs=[smem] + [vmem] * 8,
        out_specs=vmem,
        scratch_shapes=[
            pltpu.VMEM((3, cell_rows, lanes), F32),
            pltpu.VMEM((2, cells, lanes), F32),
            pltpu.VMEM((2, k1_count * (2 * box_edge + 1), grid_len), F32),
            pltpu.VMEM((2, grid_len * (2 * k1_count + 1), grid_len), F32),
            pltpu.VMEM((3, cell_rows, lanes), F32),
            pltpu.VMEM((2 * box_edge, 2 * k1_count), BF16),
            pltpu.VMEM((2, 2 * box_edge, 2 * k1_count), BF16),
            pltpu.VMEM((2 * grid_len, lanes), BF16),
            pltpu.VMEM((2, 2 * grid_len, lanes), BF16),
        ],
        compiler_params=pltpu.CompilerParams(vmem_limit_bytes=60 * 1024 * 1024),
        name="pair_terms",
    )(slab_index, boxes, kernel.reshape(grid_len * k1_count, grid_len), *tables)


def neighbours(orb_count):
    i = lax.axis_index("orb")
    core, side = lax.rem(i, 2), lax.rem(i // 2, 2)
    sibling = i + 1 - 2 * core
    across = i + 2 - 4 * side
    behind = lax.rem(i + orb_count - REACH, orb_count)
    ahead = lax.rem(i + REACH, orb_count)
    return i, core, side, sibling, across, behind, ahead


def slot_of(partner, i, side, orb_count):
    hop = jnp.minimum(lax.rem(partner - i + orb_count, orb_count), REACH)
    target = lax.rem(i, REACH) + hop
    group, place = target // REACH, lax.rem(target, REACH)
    return 2 * jnp.where(place // 2 == side, group, 2) + lax.rem(place, 2)


def remote(src, dst, send_sem, recv_sem, orb, slab):
    return pltpu.make_async_remote_copy(
        src_ref=src, dst_ref=dst, send_sem=send_sem, recv_sem=recv_sem,
        device_id=(orb, slab), device_id_type=pl.DeviceIdType.MESH,
    )


def greet(peers):
    barrier = pltpu.get_barrier_semaphore()
    for peer in peers:
        pl.semaphore_signal(barrier, inc=1, device_id=peer, device_id_type=pl.DeviceIdType.MESH)
    pl.semaphore_wait(barrier, len(peers))


def gather_kernel(
    orb_count, slab_count, chunks,
    partners_ref, offsets_ref, orbital_ref, out_ref,
    z_send, z_recv, y_send, y_recv, core_send, core_recv, own_send, own_recv, pick_send, pick_recv,
    *held,
):
    i, core, side, sibling, across, behind, ahead = neighbours(orb_count)
    s = lax.axis_index("slab")
    others = [lax.rem(s + k, slab_count) for k in range(1, slab_count)]
    rows, cells = orbital_ref.shape
    width = out_ref.shape[3] // chunks
    cols = [pl.ds(q * width, width) for q in range(chunks)]

    lane = lax.broadcasted_iota(jnp.int32, (rows, 128), 1)
    corner = jnp.zeros((rows, 128), F32)
    for c in range(3):
        corner = jnp.where(lane == c, offsets_ref[0, c].astype(F32), corner)
    out_ref[s, 0, :, pl.ds(0, cells)] = orbital_ref[...]
    out_ref[s, 0, :, pl.ds(cells, 128)] = corner.astype(BF16)
    for q in range(chunks):
        held[q][core] = out_ref[s, 0, :, cols[q]]
    greet([(p, s) for p in (sibling, across, behind, ahead)] + [(i, o) for o in others])

    z = [remote(held[q].at[core], held[q].at[2 + core], z_send.at[q], z_recv.at[q], behind, s) for q in range(chunks)]
    by_core = [
        [
            remote(held[q].at[2 * g + core], held[q].at[2 * g + core], core_send.at[g, q], core_recv.at[g, q], sibling, s)
            for q in range(chunks)
        ]
        for g in range(3)
    ]
    y_here = [remote(held[q].at[core], held[q].at[4 + core], y_send.at[q], y_recv.at[q], across, s) for q in range(chunks)]
    y_pass = [remote(held[q].at[2 + core], held[q].at[4 + core], y_send.at[q], y_recv.at[q], across, s) for q in range(chunks)]
    own = [
        remote(out_ref.at[s, 0], out_ref.at[s, 0], own_send.at[k], own_recv.at[k], i, o) for k, o in enumerate(others)
    ]
    for q in range(chunks):
        z[q].start()
    for q in range(chunks):
        pl.when(side == 1)(y_here[q].start)
    for copy in own:
        copy.start()
    for q in range(chunks):
        by_core[0][q].start()
    for q in range(chunks):
        z[q].wait_recv()
        pl.when(side == 0)(y_pass[q].start)
        by_core[1][q].start()
    slots = [slot_of(partners_ref[0, n], i, side, orb_count) for n in range(2)]
    picks = []
    for q in range(chunks):
        y_here[q].wait_recv()
        by_core[2][q].start()
        for g in range(3):
            by_core[g][q].wait_recv()
        for n in range(2):
            out_ref[s, 1 + n, :, cols[q]] = held[q][slots[n]]
            for k, o in enumerate(others):
                here = out_ref.at[s, 1 + n, :, cols[q]]
                picks.append(remote(here, here, pick_send.at[n, q, k], pick_recv.at[n, q, k], i, o))
                picks[-1].start()
    for q in range(chunks):
        z[q].wait_send()
        y_here[q].wait_send()
        for g in range(3):
            by_core[g][q].wait_send()
    for copy in own + picks:
        copy.wait()


def gather_boxes(orbitals, partners, offsets):
    orb_count, slab_count = lax.axis_size("orb"), lax.axis_size("slab")
    rows, cells = orbitals.shape[1:]
    lanes = cells + 128
    chunks = 3 if lanes % (3 * 128) == 0 else 1
    smem = pl.BlockSpec(memory_space=pltpu.SMEM)
    vmem = pl.BlockSpec(memory_space=pltpu.VMEM)
    dma = pltpu.SemaphoreType.DMA
    peers = slab_count - 1
    return pl.pallas_call(
        functools.partial(gather_kernel, orb_count, slab_count, chunks),
        out_shape=jax.ShapeDtypeStruct((slab_count, 3, rows, lanes), BF16),
        in_specs=[smem, smem, vmem],
        out_specs=vmem,
        scratch_shapes=[
            dma((chunks,)), dma((chunks,)), dma((chunks,)), dma((chunks,)),
            dma((3, chunks)), dma((3, chunks)), dma((peers,)), dma((peers,)),
            dma((2, chunks, peers)), dma((2, chunks, peers)),
        ] + [pltpu.VMEM((6, rows, lanes // chunks), BF16)] * chunks,
        compiler_params=pltpu.CompilerParams(
            collective_id=0, has_side_effects=True, vmem_limit_bytes=32 * 1024 * 1024
        ),
        name="gather_boxes",
    )(partners, offsets, orbitals.reshape(rows, cells))


def scatter_kernel(
    orb_count, slab_count, chunks,
    partners_ref, terms_ref, out_ref,
    x_send, x_recv, core_send, core_recv, y_send, y_recv, z_send, z_recv,
    from_slab, kept, to_core, from_core, to_y, from_y, to_z, from_z,
):
    i, core, side, sibling, across, behind, ahead = neighbours(orb_count)
    s = lax.axis_index("slab")
    others = [lax.rem(s + k, slab_count) for k in range(1, slab_count)]
    width = out_ref.shape[1] // chunks
    cols = [pl.ds(q * width, width) for q in range(chunks)]
    greet([(p, s) for p in (sibling, across, behind, ahead)] + [(i, o) for o in others])

    x = [
        [
            remote(terms_ref.at[o, :, :, cols[q]], from_slab.at[k, :, :, cols[q]], x_send.at[q, k], x_recv.at[q, k], i, o)
            for k, o in enumerate(others)
        ]
        for q in range(chunks)
    ]
    c = [
        remote(to_core.at[:, :, cols[q]], from_core.at[:, :, cols[q]], core_send.at[q], core_recv.at[q], sibling, s)
        for q in range(chunks)
    ]
    y = [remote(to_y.at[:, cols[q]], from_y.at[:, cols[q]], y_send.at[q], y_recv.at[q], across, s) for q in range(chunks)]
    z = [remote(to_z.at[:, cols[q]], from_z.at[:, cols[q]], z_send.at[q], z_recv.at[q], ahead, s) for q in range(chunks)]
    for q in range(chunks):
        for copy in x[q]:
            copy.start()
    slots = [slot_of(partners_ref[0, n], i, side, orb_count) for n in range(2)]

    def sum_slabs(q):
        for copy in x[q]:
            copy.wait_recv()
        total = [terms_ref[s, b, :, cols[q]].astype(F32) for b in range(3)]
        for k in range(slab_count - 1):
            total = [total[b] + from_slab[k, b, :, cols[q]].astype(F32) for b in range(3)]
        out_ref[:, cols[q]] = total[0]

        def share(slot):
            return jnp.where(slots[0] == slot, total[1], jnp.where(slots[1] == slot, total[2], 0.0))

        for g in range(3):
            to_core[g, :, cols[q]] = share(2 * g + 1 - core).astype(BF16)
        for g in range(1, 3):
            kept[g - 1, :, cols[q]] = share(2 * g + core)
        c[q].start()

    def over_core(q):
        c[q].wait_recv()
        out_ref[:, cols[q]] += from_core[0, :, cols[q]].astype(F32)
        to_y[:, cols[q]] = (kept[1, :, cols[q]] + from_core[2, :, cols[q]].astype(F32)).astype(BF16)
        y[q].start()
        kept[0, :, cols[q]] += from_core[1, :, cols[q]].astype(F32)

    def over_y(q):
        y[q].wait_recv()
        came = from_y[:, cols[q]].astype(F32)
        to_z[:, cols[q]] = (kept[0, :, cols[q]] + jnp.where(side == 0, came, 0.0)).astype(BF16)
        z[q].start()
        out_ref[:, cols[q]] += jnp.where(side == 1, came, 0.0)

    def over_z(q):
        z[q].wait_recv()
        out_ref[:, cols[q]] += from_z[:, cols[q]].astype(F32)

    stages = [sum_slabs, over_core, over_y, over_z]
    for step in range(chunks + len(stages) - 1):
        for position in reversed(range(len(stages))):
            if 0 <= step - position < chunks:
                stages[position](step - position)
    for q in range(chunks):
        for copy in x[q] + [c[q], y[q], z[q]]:
            copy.wait_send()


def scatter_terms(terms, partners):
    orb_count, slab_count = lax.axis_size("orb"), lax.axis_size("slab")
    rows, cells = terms.shape[2:]
    chunks = 4
    smem = pl.BlockSpec(memory_space=pltpu.SMEM)
    vmem = pl.BlockSpec(memory_space=pltpu.VMEM)
    dma = pltpu.SemaphoreType.DMA
    peers = slab_count - 1
    half = (rows, cells)
    return pl.pallas_call(
        functools.partial(scatter_kernel, orb_count, slab_count, chunks),
        out_shape=jax.ShapeDtypeStruct(half, F32),
        in_specs=[smem, vmem],
        out_specs=vmem,
        scratch_shapes=[dma((chunks, peers))] * 2 + [dma((chunks,))] * 6 + [
            pltpu.VMEM((peers, 3) + half, BF16),
            pltpu.VMEM((2,) + half, F32),
            pltpu.VMEM((3,) + half, BF16),
            pltpu.VMEM((3,) + half, BF16),
        ] + [pltpu.VMEM(half, BF16)] * 4,
        compiler_params=pltpu.CompilerParams(
            collective_id=1, has_side_effects=True, vmem_limit_bytes=32 * 1024 * 1024
        ),
        name="scatter_terms",
    )(partners, terms)


def per_device(orbitals, partners, offsets, kernel):
    slab_index = lax.axis_index("slab").astype(jnp.int32)
    boxes = gather_boxes(orbitals, partners, offsets)
    terms = pair_terms(boxes, slab_index[None], kernel)
    return scatter_terms(terms, partners)[None]


def solution(mesh):
    return jax.shard_map(
        per_device,
        mesh=mesh,
        in_specs=(P("orb", "slab", None), P("orb", None), P("orb", None), P(None, "slab", None)),
        out_specs=P("orb", "slab", None),
        check_vma=False,
    )
```

```python
import functools
import math

import jax
import jax.numpy as jnp
import ml_dtypes
import numpy as np
from jax import lax
from jax.experimental import pallas as pl
from jax.experimental.pallas import tpu as pltpu
from jax.sharding import PartitionSpec as P

REACH = 4
F32 = jnp.float32
BF16 = jnp.bfloat16


def phases(places, frequency, grid_len, signed):
    wrapped = (places[:, None] * frequency[None, :]) % grid_len
    angles = wrapped.astype(np.float64) * (2.0 * math.pi / grid_len)
    return np.cos(angles), signed * np.sin(angles)


def block_form(cos, sin):
    return np.block([[cos, -sin], [sin, cos]])


def make_tables(box_edge, slab_count):
    grid_len = 2 * box_edge
    half = box_edge // 2
    k1_count = grid_len // slab_count
    box = np.arange(box_edge) + half
    grid = np.arange(grid_len)
    cos, sin = phases(box, grid, grid_len, -1.0)
    f2 = np.zeros((2 * box_edge, 2 * grid_len))
    f2[:box_edge] = np.concatenate([cos, sin], 1)
    f0 = block_form(cos.T, sin.T)
    f1 = []
    e1 = []
    gcos, gsin = phases(grid, grid, grid_len, 1.0)
    for s in range(slab_count):
        mine = slice(s * k1_count, (s + 1) * k1_count)
        f1.append(block_form(cos.T[mine], sin.T[mine]))
        e1.append(block_form(gcos[:, mine], gsin[:, mine]))
    e0 = block_form(gcos, gsin)
    e2 = np.concatenate([gcos.T, -gsin.T], 0) / grid_len**3
    tables = [f2, np.stack(f1), f0, e0, np.stack(e1), e2]
    return [t.astype(np.float32).astype(ml_dtypes.bfloat16) for t in tables]


def dot(a, b):
    return jnp.dot(a, b, preferred_element_type=F32)


def neighbours(orb_count):
    i = lax.axis_index("orb")
    core, side = lax.rem(i, 2), lax.rem(i // 2, 2)
    sibling = i + 1 - 2 * core
    across = i + 2 - 4 * side
    behind = lax.rem(i + orb_count - REACH, orb_count)
    ahead = lax.rem(i + REACH, orb_count)
    return i, core, side, sibling, across, behind, ahead


def slot_of(partner, i, side, orb_count):
    hop = jnp.minimum(lax.rem(partner - i + orb_count, orb_count), REACH)
    target = lax.rem(i, REACH) + hop
    group, place = target // REACH, lax.rem(target, REACH)
    return 2 * jnp.where(place // 2 == side, group, 2) + lax.rem(place, 2)


def remote(src, dst, send_sem, recv_sem, orb, slab):
    return pltpu.make_async_remote_copy(
        src_ref=src, dst_ref=dst, send_sem=send_sem, recv_sem=recv_sem,
        device_id=(orb, slab), device_id_type=pl.DeviceIdType.MESH,
    )


def greet(peers):
    barrier = pltpu.get_barrier_semaphore()
    for peer in peers:
        pl.semaphore_signal(barrier, inc=1, device_id=peer, device_id_type=pl.DeviceIdType.MESH)
    pl.semaphore_wait(barrier, len(peers))


def gather_kernel(
    orb_count, slab_count, chunks,
    partners_ref, offsets_ref, orbital_ref, out_ref,
    z_send, z_recv, y_send, y_recv, core_send, core_recv, own_send, own_recv, pick_send, pick_recv,
    *held,
):
    i, core, side, sibling, across, behind, ahead = neighbours(orb_count)
    s = lax.axis_index("slab")
    others = [lax.rem(s + k, slab_count) for k in range(1, slab_count)]
    rows, cells = orbital_ref.shape
    width = out_ref.shape[3] // chunks
    cols = [pl.ds(q * width, width) for q in range(chunks)]

    lane = lax.broadcasted_iota(jnp.int32, (rows, 128), 1)
    corner = jnp.zeros((rows, 128), F32)
    for c in range(3):
        corner = jnp.where(lane == c, offsets_ref[0, c].astype(F32), corner)
    out_ref[s, 0, :, pl.ds(0, cells)] = orbital_ref[...]
    out_ref[s, 0, :, pl.ds(cells, 128)] = corner.astype(BF16)
    for q in range(chunks):
        held[q][core] = out_ref[s, 0, :, cols[q]]
    greet([(p, s) for p in (sibling, across, behind, ahead)] + [(i, o) for o in others])

    z = [remote(held[q].at[core], held[q].at[2 + core], z_send.at[q], z_recv.at[q], behind, s) for q in range(chunks)]
    by_core = [
        [
            remote(held[q].at[2 * g + core], held[q].at[2 * g + core], core_send.at[g, q], core_recv.at[g, q], sibling, s)
            for q in range(chunks)
        ]
        for g in range(3)
    ]
    y_here = [remote(held[q].at[core], held[q].at[4 + core], y_send.at[q], y_recv.at[q], across, s) for q in range(chunks)]
    y_pass = [remote(held[q].at[2 + core], held[q].at[4 + core], y_send.at[q], y_recv.at[q], across, s) for q in range(chunks)]
    own = [
        remote(out_ref.at[s, 0], out_ref.at[s, 0], own_send.at[k], own_recv.at[k], i, o) for k, o in enumerate(others)
    ]
    for q in range(chunks):
        z[q].start()
    for q in range(chunks):
        pl.when(side == 1)(y_here[q].start)
    for copy in own:
        copy.start()
    for q in range(chunks):
        by_core[0][q].start()
    for q in range(chunks):
        z[q].wait_recv()
        pl.when(side == 0)(y_pass[q].start)
        by_core[1][q].start()
    slots = [slot_of(partners_ref[0, n], i, side, orb_count) for n in range(2)]
    picks = []
    for q in range(chunks):
        y_here[q].wait_recv()
        by_core[2][q].start()
        for g in range(3):
            by_core[g][q].wait_recv()
        for n in range(2):
            out_ref[s, 1 + n, :, cols[q]] = held[q][slots[n]]
            for k, o in enumerate(others):
                here = out_ref.at[s, 1 + n, :, cols[q]]
                picks.append(remote(here, here, pick_send.at[n, q, k], pick_recv.at[n, q, k], i, o))
                picks[-1].start()
    for q in range(chunks):
        z[q].wait_send()
        y_here[q].wait_send()
        for g in range(3):
            by_core[g][q].wait_send()
    for copy in own + picks:
        copy.wait()


def gather_boxes(orbitals, partners, offsets):
    orb_count, slab_count = lax.axis_size("orb"), lax.axis_size("slab")
    rows, cells = orbitals.shape[1:]
    lanes = cells + 128
    chunks = 3 if lanes % (3 * 128) == 0 else 1
    smem = pl.BlockSpec(memory_space=pltpu.SMEM)
    vmem = pl.BlockSpec(memory_space=pltpu.VMEM)
    dma = pltpu.SemaphoreType.DMA
    peers = slab_count - 1
    return pl.pallas_call(
        functools.partial(gather_kernel, orb_count, slab_count, chunks),
        out_shape=jax.ShapeDtypeStruct((slab_count, 3, rows, lanes), BF16),
        in_specs=[smem, smem, vmem],
        out_specs=vmem,
        scratch_shapes=[
            dma((chunks,)), dma((chunks,)), dma((chunks,)), dma((chunks,)),
            dma((3, chunks)), dma((3, chunks)), dma((peers,)), dma((peers,)),
            dma((2, chunks, peers)), dma((2, chunks, peers)),
        ] + [pltpu.VMEM((6, rows, lanes // chunks), BF16)] * chunks,
        compiler_params=pltpu.CompilerParams(
            collective_id=0, has_side_effects=True, vmem_limit_bytes=32 * 1024 * 1024
        ),
        name="gather_boxes",
    )(partners, offsets, orbitals.reshape(rows, cells))


def pair_kernel(
    orb_count, box_edge, k1_count,
    partners_ref, boxes_ref, kernel_ref, f2_ref, f1_ref, f0_ref, e0_ref, e1_ref, e2_ref,
    out_ref,
    cells, here, y_parts, v_parts, k_rows, terms, e1_own, e1_far, e2_own, e2_far,
    x_send, x_recv, core_send, core_recv, y_send, y_recv, z_send, z_recv,
    packed, from_slab, kept, to_core, from_core, to_y, from_y, to_z, from_z,
):
    edge = box_edge
    grid_len = 2 * edge
    half = edge // 2
    lanes = 2 * edge
    slab_count, _, rows, _ = boxes_ref.shape
    i, core, side, sibling, across, behind, ahead = neighbours(orb_count)
    slab = lax.axis_index("slab")
    others = [lax.rem(slab + k, slab_count) for k in range(1, slab_count)]
    greet([(p, slab) for p in (sibling, across, behind, ahead)] + [(i, o) for o in others])

    lane = lax.broadcasted_iota(jnp.int32, (edge, lanes), 1)
    low_lanes = lane < edge
    row = lax.broadcasted_iota(jnp.int32, (edge, lanes), 0)
    corner_lane = lax.broadcasted_iota(jnp.int32, (1, lanes), 1)

    def corner(b):
        held = boxes_ref[0, b, :, pl.ds(edge * edge, lanes)].astype(F32)[0:1]
        return [jnp.sum(jnp.where(corner_lane == c, held, 0.0)).astype(jnp.int32) for c in range(3)]

    corners = [corner(b) for b in range(3)]
    shifts = [[corners[1 + n][c] - corners[0][c] for c in range(3)] for n in range(2)]
    cell_pitch = edge + 1
    y_pitch = 2 * edge + 1
    v_pitch = 2 * k1_count + 1
    k_pitch = k1_count + 1

    e1_grid = e1_ref[slab]
    e2_grid = e2_ref[...]
    sel_lane = lax.broadcasted_iota(jnp.int32, (grid_len, lanes), 1)
    sel_row = lax.broadcasted_iota(jnp.int32, (grid_len, lanes), 0)

    def windows(d1, d2):
        pick_rows = (row + half + d1 == lane).astype(F32).astype(BF16)
        top = dot(pick_rows, e1_grid[:grid_len]).astype(BF16)
        bottom = dot(pick_rows, e1_grid[grid_len:]).astype(BF16)
        pick_cols = ((sel_lane + half + d2 == sel_row) & (sel_lane < edge)).astype(F32).astype(BF16)
        return jnp.concatenate([top, bottom], 0), dot(e2_grid, pick_cols).astype(BF16)

    e1_own[...], e2_own[...] = windows(0, 0)
    for n in range(2):
        e1_far[n], e2_far[n] = windows(shifts[n][1], shifts[n][2])

    def unpack(g, carry):
        lo_at = pl.ds(2 * g, edge, stride=cell_pitch)
        hi_at = pl.ds(2 * g + 1, edge, stride=cell_pitch)
        for b in range(3):
            both = boxes_ref[:, b, :, pl.ds(pl.multiple_of(g * lanes, lanes), lanes)].astype(F32)
            both = both.reshape(edge, lanes)
            cells[b, lo_at, :] = jnp.where(low_lanes, both, 0.0)
            cells[b, hi_at, :] = jnp.where(low_lanes, pltpu.roll(both, edge, 1), 0.0)
        for k in range(4):
            k0 = 4 * g + k
            k_rows[pl.ds(k0 * k_pitch, k1_count), :] = kernel_ref[pl.ds(pl.multiple_of(k0 * k1_count, k1_count), k1_count), :]
        return carry

    lax.fori_loop(0, edge // 2, unpack, 0, unroll=2)

    def moved(b, c0, d0, d1, d2):
        source = c0 + d0
        at = jnp.clip(source, 0, edge - 1)
        block = cells[b, pl.ds(at * cell_pitch, edge), :]
        block = pltpu.roll(block, (-d2) & (lanes - 1), 1)
        block = pltpu.roll(block, (-d1) & (edge - 1), 0)
        inside = (row + d1 >= 0) & (row + d1 < edge) & (source >= 0) & (source < edge)
        return jnp.where(inside, block, 0.0)

    batch = 4

    def forward(step, carry):
        z = []
        for j in range(batch):
            c0 = step * batch + j
            own = cells[0, pl.ds(c0 * cell_pitch, edge), :]
            for n in range(2):
                d0, d1, d2 = shifts[n]
                partner = moved(1 + n, c0, -d0, -d1, -d2)
                here[n, pl.ds(pl.multiple_of(c0 * edge, edge), edge), :] = partner
                z.append((own * partner).astype(BF16))
        z = dot(jnp.concatenate(z, 0), f2_ref[...]).astype(BF16)
        for j in range(batch):
            c0 = step * batch + j
            mine = [z[(2 * j + n) * edge : (2 * j + n + 1) * edge] for n in range(2)]
            mine = jnp.concatenate(
                [jnp.concatenate([m[:, :grid_len], m[:, grid_len:]], 0) for m in mine], 1
            )
            y = dot(f1_ref[slab], mine)
            for n in range(2):
                part = y[:, n * grid_len : (n + 1) * grid_len]
                y_parts[n, pl.ds(c0, k1_count, stride=y_pitch), :] = part[:k1_count]
                y_parts[n, pl.ds(edge + c0, k1_count, stride=y_pitch), :] = part[k1_count:]
        return carry

    lax.fori_loop(0, edge // batch, forward, 0)

    def middle(k1, carry):
        at = pl.ds(k1 * y_pitch, 2 * edge)
        y = jnp.concatenate([y_parts[n, at, :].astype(BF16) for n in range(2)], 1)
        x = dot(f0_ref[...], y)
        k = k_rows[pl.ds(k1, grid_len, stride=k_pitch), :]
        k = jnp.concatenate([k, k], 1)
        w = jnp.concatenate([(x[:grid_len] * k).astype(BF16), (x[grid_len:] * k).astype(BF16)], 0)
        v = dot(e0_ref[...], w)
        for n in range(2):
            part = v[:, n * grid_len : (n + 1) * grid_len]
            v_parts[n, pl.ds(k1, grid_len, stride=v_pitch), :] = part[:grid_len]
            v_parts[n, pl.ds(k1_count + k1, grid_len, stride=v_pitch), :] = part[grid_len:]
        return carry

    lax.fori_loop(0, k1_count, middle, 0, unroll=4)

    def v_rows(n, u0):
        u0 = jnp.clip(u0, 0, grid_len - 1)
        return v_parts[n, pl.ds(u0 * v_pitch, 2 * k1_count), :].astype(BF16)

    piece = packed.shape[2]
    pieces = rows // piece
    parts = 2
    width = edge * edge // parts
    cols = [pl.ds(h * width, width) for h in range(parts)]

    def slab_copies(number):
        to = lax.rem(slab + 1 + number // pieces, slab_count)
        return [
            remote(
                packed.at[number, :, :, cols[h]], from_slab.at[number, :, :, cols[h]],
                x_send.at[number, h], x_recv.at[number, h], i, to,
            )
            for h in range(parts)
        ]

    def one_piece(number, carry):
        target = lax.rem(slab + 1 + number // pieces, slab_count)
        first = target * rows + lax.rem(number, pieces) * piece

        def backward(step, inner):
            u = []
            for j in range(batch):
                c0 = first + step * batch + j
                v = jnp.concatenate([v_rows(n, half + c0) for n in range(2)], 1)
                part = dot(e1_own[...], v).astype(BF16)
                for n in range(2):
                    mine = part[:, n * grid_len : (n + 1) * grid_len]
                    u.append(jnp.concatenate([mine[:edge], mine[edge:]], 1))
            field = dot(jnp.concatenate(u, 0), e2_own[...])
            for j in range(batch):
                c0 = first + step * batch + j
                at = pl.ds(pl.multiple_of(c0 * edge, edge), edge)
                own = field[2 * j * edge : (2 * j + 1) * edge] * here[0, at, :]
                own += field[(2 * j + 1) * edge : (2 * j + 2) * edge] * here[1, at, :]
                terms[0, pl.ds((step * batch + j) * cell_pitch, edge), :] = own
            for n in range(2):
                d0, d1, d2 = shifts[n]
                u = []
                for j in range(batch):
                    mine = dot(e1_far[n], v_rows(n, half + d0 + first + step * batch + j)).astype(BF16)
                    u.append(jnp.concatenate([mine[:edge], mine[edge:]], 1))
                field = dot(jnp.concatenate(u, 0), e2_far[n])
                for j in range(batch):
                    there = moved(0, first + step * batch + j, d0, d1, d2)
                    to = pl.ds((step * batch + j) * cell_pitch, edge)
                    terms[1 + n, to, :] = field[j * edge : (j + 1) * edge] * there
            return inner

        lax.fori_loop(0, piece // batch, backward, 0)

        def pack(g, inner):
            for b in range(3):
                lo = terms[b, pl.ds(2 * g, piece, stride=cell_pitch), :]
                hi = terms[b, pl.ds(2 * g + 1, piece, stride=cell_pitch), :]
                both = lo + pltpu.roll(hi, edge, 1)
                packed[number, b, :, pl.ds(pl.multiple_of(g * lanes, lanes), lanes)] = both.astype(BF16)
            return inner

        lax.fori_loop(0, edge // 2, pack, 0, unroll=4)

        @pl.when(number < (slab_count - 1) * pieces)
        def _():
            for copy in slab_copies(number):
                copy.start()

        return carry

    lax.fori_loop(0, slab_count * pieces, one_piece, 0)

    slots = [slot_of(partners_ref[0, n], i, side, orb_count) for n in range(2)]
    steps = [(q, h) for q in range(pieces) for h in range(parts)]
    c = [
        remote(to_core.at[q, :, :, cols[h]], from_core.at[q, :, :, cols[h]], core_send.at[q, h], core_recv.at[q, h], sibling, slab)
        for q, h in steps
    ]
    y = [remote(to_y.at[q, :, cols[h]], from_y.at[q, :, cols[h]], y_send.at[q, h], y_recv.at[q, h], across, slab) for q, h in steps]
    z = [remote(to_z.at[q, :, cols[h]], from_z.at[q, :, cols[h]], z_send.at[q, h], z_recv.at[q, h], ahead, slab) for q, h in steps]

    def sum_slabs(t):
        q, h = steps[t]
        at = pl.ds(q * piece, piece)
        total = [packed[(slab_count - 1) * pieces + q, b, :, cols[h]].astype(F32) for b in range(3)]
        for k in range(slab_count - 1):
            slab_copies(k * pieces + q)[h].wait_recv()
            total = [total[b] + from_slab[k * pieces + q, b, :, cols[h]].astype(F32) for b in range(3)]
        out_ref[at, cols[h]] = total[0]

        def share(slot):
            return jnp.where(slots[0] == slot, total[1], jnp.where(slots[1] == slot, total[2], 0.0))

        for g in range(3):
            to_core[q, g, :, cols[h]] = share(2 * g + 1 - core).astype(BF16)
        c[t].start()
        for g in range(1, 3):
            kept[q, g - 1, :, cols[h]] = share(2 * g + core)

    def over_core(t):
        q, h = steps[t]
        at = pl.ds(q * piece, piece)
        c[t].wait_recv()
        to_y[q, :, cols[h]] = (kept[q, 1, :, cols[h]] + from_core[q, 2, :, cols[h]].astype(F32)).astype(BF16)
        y[t].start()
        out_ref[at, cols[h]] += from_core[q, 0, :, cols[h]].astype(F32)
        kept[q, 0, :, cols[h]] += from_core[q, 1, :, cols[h]].astype(F32)

    def over_y(t):
        q, h = steps[t]
        at = pl.ds(q * piece, piece)
        y[t].wait_recv()
        came = from_y[q, :, cols[h]].astype(F32)
        to_z[q, :, cols[h]] = (kept[q, 0, :, cols[h]] + jnp.where(side == 0, came, 0.0)).astype(BF16)
        z[t].start()
        out_ref[at, cols[h]] += jnp.where(side == 1, came, 0.0)

    def over_z(t):
        q, h = steps[t]
        at = pl.ds(q * piece, piece)
        z[t].wait_recv()
        out_ref[at, cols[h]] += from_z[q, :, cols[h]].astype(F32)

    stages = [sum_slabs, over_core, over_y, over_z]
    for step in range(len(steps) + len(stages) - 1):
        for position in reversed(range(len(stages))):
            if 0 <= step - position < len(steps):
                stages[position](step - position)
    for number in range((slab_count - 1) * pieces):
        for copy in slab_copies(number):
            copy.wait_send()
    for copy in c + y + z:
        copy.wait_send()


def pair_terms(boxes, partners, kernel):
    orb_count = lax.axis_size("orb")
    slab_count, _, rows, _ = boxes.shape
    box_edge = slab_count * rows
    grid_len, k1_count = kernel.shape[0], kernel.shape[1]
    tables = make_tables(box_edge, slab_count)
    smem = pl.BlockSpec(memory_space=pltpu.SMEM)
    vmem = pl.BlockSpec(memory_space=pltpu.VMEM)
    cells = box_edge * box_edge
    cell_rows = box_edge * (box_edge + 1)
    lanes = 2 * box_edge
    piece = min(rows, 16)
    pieces = rows // piece
    sent = (slab_count - 1) * pieces
    flat = (piece, cells)
    dma = pltpu.SemaphoreType.DMA
    return pl.pallas_call(
        functools.partial(pair_kernel, orb_count, box_edge, k1_count),
        out_shape=jax.ShapeDtypeStruct((rows, cells), F32),
        in_specs=[smem] + [vmem] * 8,
        out_specs=vmem,
        scratch_shapes=[
            pltpu.VMEM((3, cell_rows, lanes), F32),
            pltpu.VMEM((2, cells, lanes), F32),
            pltpu.VMEM((2, k1_count * (2 * box_edge + 1), grid_len), F32),
            pltpu.VMEM((2, grid_len * (2 * k1_count + 1), grid_len), F32),
            pltpu.VMEM((grid_len * (k1_count + 1), grid_len), F32),
            pltpu.VMEM((3, piece * (box_edge + 1), lanes), F32),
            pltpu.VMEM((2 * box_edge, 2 * k1_count), BF16),
            pltpu.VMEM((2, 2 * box_edge, 2 * k1_count), BF16),
            pltpu.VMEM((2 * grid_len, lanes), BF16),
            pltpu.VMEM((2, 2 * grid_len, lanes), BF16),
        ] + [dma((sent, 2))] * 2 + [dma((pieces, 2))] * 6 + [
            pltpu.VMEM((slab_count * pieces, 3) + flat, BF16),
            pltpu.VMEM((sent, 3) + flat, BF16),
            pltpu.VMEM((pieces, 2) + flat, F32),
            pltpu.VMEM((pieces, 3) + flat, BF16),
            pltpu.VMEM((pieces, 3) + flat, BF16),
        ] + [pltpu.VMEM((pieces,) + flat, BF16)] * 4,
        compiler_params=pltpu.CompilerParams(
            collective_id=1, has_side_effects=True, vmem_limit_bytes=60 * 1024 * 1024
        ),
        name="pair_terms",
    )(partners, boxes, kernel.reshape(grid_len * k1_count, grid_len), *tables)


def per_device(orbitals, partners, offsets, kernel):
    boxes = gather_boxes(orbitals, partners, offsets)
    return pair_terms(boxes, partners, kernel)[None]


def solution(mesh):
    return jax.shard_map(
        per_device,
        mesh=mesh,
        in_specs=(P("orb", "slab", None), P("orb", None), P("orb", None), P(None, "slab", None)),
        out_specs=P("orb", "slab", None),
        check_vma=False,
    )
```

```python
import functools
import math

import jax
import jax.numpy as jnp
import ml_dtypes
import numpy as np
from jax import lax
from jax.experimental import pallas as pl
from jax.experimental.pallas import tpu as pltpu
from jax.sharding import PartitionSpec as P

REACH = 4
F32 = jnp.float32
BF16 = jnp.bfloat16


def phases(places, frequency, grid_len, signed):
    wrapped = (places[:, None] * frequency[None, :]) % grid_len
    angles = wrapped.astype(np.float64) * (2.0 * math.pi / grid_len)
    return np.cos(angles), signed * np.sin(angles)


def block_form(cos, sin):
    return np.block([[cos, -sin], [sin, cos]])


def make_tables(box_edge, slab_count):
    grid_len = 2 * box_edge
    half = box_edge // 2
    k1_count = grid_len // slab_count
    box = np.arange(box_edge) + half
    grid = np.arange(grid_len)
    cos, sin = phases(box, grid, grid_len, -1.0)
    f2 = np.zeros((2 * box_edge, 2 * grid_len))
    f2[:box_edge] = np.concatenate([cos, sin], 1)
    f0 = block_form(cos.T, sin.T)
    f1 = []
    e1 = []
    gcos, gsin = phases(grid, grid, grid_len, 1.0)
    for s in range(slab_count):
        mine = slice(s * k1_count, (s + 1) * k1_count)
        f1.append(block_form(cos.T[mine], sin.T[mine]))
        e1.append(block_form(gcos[:, mine], gsin[:, mine]))
    e0 = block_form(gcos, gsin)
    e2 = np.concatenate([gcos.T, -gsin.T], 0) / grid_len**3
    tables = [f2, np.stack(f1), f0, e0, np.stack(e1), e2]
    return [t.astype(np.float32).astype(ml_dtypes.bfloat16) for t in tables]


def dot(a, b):
    return jnp.dot(a, b, preferred_element_type=F32)


def neighbours(orb_count):
    i = lax.axis_index("orb")
    core, side = lax.rem(i, 2), lax.rem(i // 2, 2)
    sibling = i + 1 - 2 * core
    across = i + 2 - 4 * side
    behind = lax.rem(i + orb_count - REACH, orb_count)
    ahead = lax.rem(i + REACH, orb_count)
    return i, core, side, sibling, across, behind, ahead


def slot_of(partner, i, side, orb_count):
    hop = jnp.minimum(lax.rem(partner - i + orb_count, orb_count), REACH)
    target = lax.rem(i, REACH) + hop
    group, place = target // REACH, lax.rem(target, REACH)
    return 2 * jnp.where(place // 2 == side, group, 2) + lax.rem(place, 2)


def remote(src, dst, send_sem, recv_sem, orb, slab):
    return pltpu.make_async_remote_copy(
        src_ref=src, dst_ref=dst, send_sem=send_sem, recv_sem=recv_sem,
        device_id=(orb, slab), device_id_type=pl.DeviceIdType.MESH,
    )


def greet(peers):
    barrier = pltpu.get_barrier_semaphore()
    for peer in peers:
        pl.semaphore_signal(barrier, inc=1, device_id=peer, device_id_type=pl.DeviceIdType.MESH)
    pl.semaphore_wait(barrier, len(peers))


def gather_kernel(
    orb_count, slab_count, chunks,
    partners_ref, offsets_ref, orbital_ref, out_ref,
    x_send, x_recv, z_send, z_recv, y_send, y_recv, core_send, core_recv,
    *held,
):
    i, core, side, sibling, across, behind, ahead = neighbours(orb_count)
    s = lax.axis_index("slab")
    others = [lax.rem(s + k, slab_count) for k in range(slab_count)]
    rows, cells = orbital_ref.shape
    width = out_ref.shape[3] // chunks
    cols = [pl.ds(q * width, width) for q in range(chunks)]

    lane = lax.broadcasted_iota(jnp.int32, (rows, 128), 1)
    corner = jnp.zeros((rows, 128), F32)
    for c in range(3):
        corner = jnp.where(lane == c, offsets_ref[0, c].astype(F32), corner)
    out_ref[s, 0, :, pl.ds(0, cells)] = orbital_ref[...]
    out_ref[s, 0, :, pl.ds(cells, 128)] = corner.astype(BF16)
    for q in range(chunks):
        held[q][core] = out_ref[s, 0, :, cols[q]]
    greet([(p, s) for p in (sibling, across, behind, ahead)] + [(i, o) for o in others[1:]])

    units = slab_count * chunks

    def along(u, source, target, send, recv, to):
        return remote(held[u].at[source], held[u].at[target], send, recv, to, s)

    x = [
        remote(held[q].at[core], held[(slab_count - k) * chunks + q].at[core], x_send.at[k, q], x_recv.at[k, q], i, others[k])
        for k in range(1, slab_count)
        for q in range(chunks)
    ]
    x_came = [
        remote(held[q].at[core], held[k * chunks + q].at[core], x_send.at[slab_count - k, q], x_recv.at[slab_count - k, q], i, others[k])
        for k in range(1, slab_count)
        for q in range(chunks)
    ]
    z = [along(u, core, 2 + core, z_send.at[u], z_recv.at[u], behind) for u in range(units)]
    y_here = [along(u, core, 4 + core, y_send.at[u], y_recv.at[u], across) for u in range(units)]
    y_pass = [along(u, 2 + core, 4 + core, y_send.at[u], y_recv.at[u], across) for u in range(units)]
    by_core = [
        [along(u, 2 * g + core, 2 * g + core, core_send.at[g, u], core_recv.at[g, u], sibling) for u in range(units)]
        for g in range(3)
    ]
    slots = [slot_of(partners_ref[0, n], i, side, orb_count) for n in range(2)]

    def send_own(u):
        if u >= chunks:
            x_came[u - chunks].wait_recv()
        z[u].start()
        pl.when(side == 1)(y_here[u].start)
        by_core[0][u].start()
        if u >= chunks:
            out_ref[others[u // chunks], 0, :, cols[u % chunks]] = held[u][core]

    def pass_on(u):
        z[u].wait_recv()
        pl.when(side == 0)(y_pass[u].start)
        by_core[1][u].start()

    def pass_last(u):
        y_here[u].wait_recv()
        by_core[2][u].start()

    def pick(u):
        for g in range(3):
            by_core[g][u].wait_recv()
        for n in range(2):
            out_ref[others[u // chunks], 1 + n, :, cols[u % chunks]] = held[u][slots[n]]

    for copy in x:
        copy.start()
    stages = [(send_own, 0), (pass_on, chunks), (pass_last, chunks + 1), (pick, chunks + 2)]
    for step in range(units + chunks + 2):
        for stage, lag in stages:
            if 0 <= step - lag < units:
                stage(step - lag)
    for copy in x + z + y_here + by_core[0] + by_core[1] + by_core[2]:
        copy.wait_send()


def gather_boxes(orbitals, partners, offsets):
    orb_count, slab_count = lax.axis_size("orb"), lax.axis_size("slab")
    rows, cells = orbitals.shape[1:]
    lanes = cells + 128
    chunks = 3 if lanes % (3 * 128) == 0 else 1
    smem = pl.BlockSpec(memory_space=pltpu.SMEM)
    vmem = pl.BlockSpec(memory_space=pltpu.VMEM)
    dma = pltpu.SemaphoreType.DMA
    units = slab_count * chunks
    return pl.pallas_call(
        functools.partial(gather_kernel, orb_count, slab_count, chunks),
        out_shape=jax.ShapeDtypeStruct((slab_count, 3, rows, lanes), BF16),
        in_specs=[smem, smem, vmem],
        out_specs=vmem,
        scratch_shapes=[
            dma((slab_count, chunks)), dma((slab_count, chunks)), dma((units,)), dma((units,)), dma((units,)), dma((units,)),
            dma((3, units)), dma((3, units)),
        ] + [pltpu.VMEM((6, rows, lanes // chunks), BF16)] * units,
        compiler_params=pltpu.CompilerParams(
            collective_id=0, has_side_effects=True, vmem_limit_bytes=32 * 1024 * 1024
        ),
        name="gather_boxes",
    )(partners, offsets, orbitals.reshape(rows, cells))


def pair_kernel(
    orb_count, box_edge, k1_count,
    partners_ref, boxes_ref, kernel_ref, f2_ref, f1_ref, f0_ref, e0_ref, e1_ref, e2_ref,
    out_ref,
    cells, here, y_parts, v_parts, k_rows, terms, e1_own, e1_far, e2_own, e2_far,
    x_send, x_recv, core_send, core_recv, y_send, y_recv, z_send, z_recv,
    own_terms, kept, to_core, from_core, to_y, from_y, to_z, from_z, to_x, from_x,
):
    edge = box_edge
    grid_len = 2 * edge
    half = edge // 2
    lanes = 2 * edge
    slab_count, _, rows, _ = boxes_ref.shape
    i, core, side, sibling, across, behind, ahead = neighbours(orb_count)
    slab = lax.axis_index("slab")
    others = [lax.rem(slab + k, slab_count) for k in range(1, slab_count)]
    greet([(p, slab) for p in (sibling, across, behind, ahead)] + [(i, o) for o in others])

    lane = lax.broadcasted_iota(jnp.int32, (edge, lanes), 1)
    low_lanes = lane < edge
    row = lax.broadcasted_iota(jnp.int32, (edge, lanes), 0)
    corner_lane = lax.broadcasted_iota(jnp.int32, (1, lanes), 1)

    def corner(b):
        held = boxes_ref[0, b, :, pl.ds(edge * edge, lanes)].astype(F32)[0:1]
        return [jnp.sum(jnp.where(corner_lane == c, held, 0.0)).astype(jnp.int32) for c in range(3)]

    corners = [corner(b) for b in range(3)]
    shifts = [[corners[1 + n][c] - corners[0][c] for c in range(3)] for n in range(2)]
    cell_pitch = edge + 1
    y_pitch = 2 * edge + 1
    v_pitch = 2 * k1_count + 1
    k_pitch = k1_count + 1

    e1_grid = e1_ref[slab]
    e2_grid = e2_ref[...]
    sel_lane = lax.broadcasted_iota(jnp.int32, (grid_len, lanes), 1)
    sel_row = lax.broadcasted_iota(jnp.int32, (grid_len, lanes), 0)

    def windows(d1, d2):
        pick_rows = (row + half + d1 == lane).astype(F32).astype(BF16)
        top = dot(pick_rows, e1_grid[:grid_len]).astype(BF16)
        bottom = dot(pick_rows, e1_grid[grid_len:]).astype(BF16)
        pick_cols = ((sel_lane + half + d2 == sel_row) & (sel_lane < edge)).astype(F32).astype(BF16)
        return jnp.concatenate([top, bottom], 0), dot(e2_grid, pick_cols).astype(BF16)

    e1_own[...], e2_own[...] = windows(0, 0)
    for n in range(2):
        e1_far[n], e2_far[n] = windows(shifts[n][1], shifts[n][2])

    def unpack(g, carry):
        lo_at = pl.ds(2 * g, edge, stride=cell_pitch)
        hi_at = pl.ds(2 * g + 1, edge, stride=cell_pitch)
        for b in range(3):
            both = boxes_ref[:, b, :, pl.ds(pl.multiple_of(g * lanes, lanes), lanes)].astype(F32)
            both = both.reshape(edge, lanes)
            cells[b, lo_at, :] = jnp.where(low_lanes, both, 0.0)
            cells[b, hi_at, :] = jnp.where(low_lanes, pltpu.roll(both, edge, 1), 0.0)
        for k in range(4):
            k0 = 4 * g + k
            k_rows[pl.ds(k0 * k_pitch, k1_count), :] = kernel_ref[pl.ds(pl.multiple_of(k0 * k1_count, k1_count), k1_count), :]
        return carry

    lax.fori_loop(0, edge // 2, unpack, 0, unroll=2)

    def moved(b, c0, d0, d1, d2):
        source = c0 + d0
        at = jnp.clip(source, 0, edge - 1)
        block = cells[b, pl.ds(at * cell_pitch, edge), :]
        block = pltpu.roll(block, (-d2) & (lanes - 1), 1)
        block = pltpu.roll(block, (-d1) & (edge - 1), 0)
        inside = (row + d1 >= 0) & (row + d1 < edge) & (source >= 0) & (source < edge)
        return jnp.where(inside, block, 0.0)

    batch = 4

    def forward(step, carry):
        z = []
        for j in range(batch):
            c0 = step * batch + j
            own = cells[0, pl.ds(c0 * cell_pitch, edge), :]
            for n in range(2):
                d0, d1, d2 = shifts[n]
                partner = moved(1 + n, c0, -d0, -d1, -d2)
                here[n, pl.ds(pl.multiple_of(c0 * edge, edge), edge), :] = partner
                z.append((own * partner).astype(BF16))
        z = dot(jnp.concatenate(z, 0), f2_ref[...]).astype(BF16)
        for j in range(batch):
            c0 = step * batch + j
            mine = [z[(2 * j + n) * edge : (2 * j + n + 1) * edge] for n in range(2)]
            mine = jnp.concatenate(
                [jnp.concatenate([m[:, :grid_len], m[:, grid_len:]], 0) for m in mine], 1
            )
            y = dot(f1_ref[slab], mine)
            for n in range(2):
                part = y[:, n * grid_len : (n + 1) * grid_len]
                y_parts[n, pl.ds(c0, k1_count, stride=y_pitch), :] = part[:k1_count]
                y_parts[n, pl.ds(edge + c0, k1_count, stride=y_pitch), :] = part[k1_count:]
        return carry

    lax.fori_loop(0, edge // batch, forward, 0)

    def middle(k1, carry):
        at = pl.ds(k1 * y_pitch, 2 * edge)
        y = jnp.concatenate([y_parts[n, at, :].astype(BF16) for n in range(2)], 1)
        x = dot(f0_ref[...], y)
        k = k_rows[pl.ds(k1, grid_len, stride=k_pitch), :]
        k = jnp.concatenate([k, k], 1)
        w = jnp.concatenate([(x[:grid_len] * k).astype(BF16), (x[grid_len:] * k).astype(BF16)], 0)
        v = dot(e0_ref[...], w)
        for n in range(2):
            part = v[:, n * grid_len : (n + 1) * grid_len]
            v_parts[n, pl.ds(k1, grid_len, stride=v_pitch), :] = part[:grid_len]
            v_parts[n, pl.ds(k1_count + k1, grid_len, stride=v_pitch), :] = part[grid_len:]
        return carry

    lax.fori_loop(0, k1_count, middle, 0, unroll=4)

    def v_rows(n, u0):
        u0 = jnp.clip(u0, 0, grid_len - 1)
        return v_parts[n, pl.ds(u0 * v_pitch, 2 * k1_count), :].astype(BF16)

    piece = own_terms.shape[1]
    pieces = rows // piece
    numbers = slab_count * pieces
    away = numbers - pieces
    slots = [slot_of(partners_ref[0, n], i, side, orb_count) for n in range(2)]

    def over_core(t):
        return remote(to_core.at[t], from_core.at[t], core_send.at[t], core_recv.at[t], sibling, slab)

    def over_y(t):
        return remote(to_y.at[t], from_y.at[t], y_send.at[t], y_recv.at[t], across, slab)

    def over_z(t):
        return remote(to_z.at[t], from_z.at[t], z_send.at[t], z_recv.at[t], ahead, slab)

    def over_x(t):
        target = lax.rem(slab + 1 + t // pieces, slab_count)
        return remote(to_x.at[t], from_x.at[t], x_send.at[t], x_recv.at[t], i, target)

    def compute(number):
        target = lax.rem(slab + 1 + number // pieces, slab_count)
        first = target * rows + lax.rem(number, pieces) * piece

        def backward(step, inner):
            u = []
            for j in range(batch):
                c0 = first + step * batch + j
                v = jnp.concatenate([v_rows(n, half + c0) for n in range(2)], 1)
                part = dot(e1_own[...], v).astype(BF16)
                for n in range(2):
                    mine = part[:, n * grid_len : (n + 1) * grid_len]
                    u.append(jnp.concatenate([mine[:edge], mine[edge:]], 1))
            field = dot(jnp.concatenate(u, 0), e2_own[...])
            for j in range(batch):
                c0 = first + step * batch + j
                at = pl.ds(pl.multiple_of(c0 * edge, edge), edge)
                own = field[2 * j * edge : (2 * j + 1) * edge] * here[0, at, :]
                own += field[(2 * j + 1) * edge : (2 * j + 2) * edge] * here[1, at, :]
                terms[0, pl.ds((step * batch + j) * cell_pitch, edge), :] = own
            for n in range(2):
                d0, d1, d2 = shifts[n]
                u = []
                for j in range(batch):
                    mine = dot(e1_far[n], v_rows(n, half + d0 + first + step * batch + j)).astype(BF16)
                    u.append(jnp.concatenate([mine[:edge], mine[edge:]], 1))
                field = dot(jnp.concatenate(u, 0), e2_far[n])
                for j in range(batch):
                    there = moved(0, first + step * batch + j, d0, d1, d2)
                    to = pl.ds((step * batch + j) * cell_pitch, edge)
                    terms[1 + n, to, :] = field[j * edge : (j + 1) * edge] * there
            return inner

        lax.fori_loop(0, piece // batch, backward, 0)

        def pack(g, inner):
            at = pl.ds(pl.multiple_of(g * lanes, lanes), lanes)
            both = []
            for b in range(3):
                lo = terms[b, pl.ds(2 * g, piece, stride=cell_pitch), :]
                hi = terms[b, pl.ds(2 * g + 1, piece, stride=cell_pitch), :]
                both.append(lo + pltpu.roll(hi, edge, 1))
            own_terms[number, :, at] = both[0]

            def share(slot):
                return jnp.where(slots[0] == slot, both[1], jnp.where(slots[1] == slot, both[2], 0.0))

            for group in range(3):
                to_core[number, group, :, at] = share(2 * group + 1 - core).astype(BF16)
            for group in range(1, 3):
                kept[number, group - 1, :, at] = share(2 * group + core)
            return inner

        lax.fori_loop(0, edge // 2, pack, 0, unroll=4)
        over_core(number).start()

    def after_core(t):
        over_core(t).wait_recv()
        to_y[t] = (kept[t, 1] + from_core[t, 2].astype(F32)).astype(BF16)
        over_y(t).start()
        own_terms[t] += from_core[t, 0].astype(F32)
        kept[t, 0] += from_core[t, 1].astype(F32)

    def after_y(t):
        over_y(t).wait_recv()
        came = from_y[t].astype(F32)
        to_z[t] = (kept[t, 0] + jnp.where(side == 0, came, 0.0)).astype(BF16)
        over_z(t).start()
        own_terms[t] += jnp.where(side == 1, came, 0.0)

    def after_z(t):
        over_z(t).wait_recv()
        own_terms[t] += from_z[t].astype(F32)

        @pl.when(t < away)
        def _():
            to_x[t] = own_terms[t].astype(BF16)
            over_x(t).start()

    def one_step(step, carry):
        for stage, lag in ((after_core, 1), (after_y, 2), (after_z, 3), (compute, 0)):
            pl.when((step >= lag) & (step < numbers + lag))(functools.partial(stage, step - lag))
        return carry

    lax.fori_loop(0, numbers + 3, one_step, 0)

    for q in range(pieces):
        total = own_terms[away + q]
        for k in range(slab_count - 1):
            over_x(k * pieces + q).wait_recv()
            total += from_x[k * pieces + q].astype(F32)
        out_ref[pl.ds(q * piece, piece), :] = total
    for t in range(numbers):
        over_core(t).wait_send()
        over_y(t).wait_send()
        over_z(t).wait_send()
        if t < away:
            over_x(t).wait_send()


def pair_terms(boxes, partners, kernel):
    orb_count = lax.axis_size("orb")
    slab_count, _, rows, _ = boxes.shape
    box_edge = slab_count * rows
    grid_len, k1_count = kernel.shape[0], kernel.shape[1]
    tables = make_tables(box_edge, slab_count)
    smem = pl.BlockSpec(memory_space=pltpu.SMEM)
    vmem = pl.BlockSpec(memory_space=pltpu.VMEM)
    cells = box_edge * box_edge
    cell_rows = box_edge * (box_edge + 1)
    lanes = 2 * box_edge
    piece = min(rows, 16)
    pieces = rows // piece
    numbers = slab_count * pieces
    sent = numbers - pieces
    flat = (piece, cells)
    dma = pltpu.SemaphoreType.DMA
    return pl.pallas_call(
        functools.partial(pair_kernel, orb_count, box_edge, k1_count),
        out_shape=jax.ShapeDtypeStruct((rows, cells), F32),
        in_specs=[smem] + [vmem] * 8,
        out_specs=vmem,
        scratch_shapes=[
            pltpu.VMEM((3, cell_rows, lanes), F32),
            pltpu.VMEM((2, cells, lanes), F32),
            pltpu.VMEM((2, k1_count * (2 * box_edge + 1), grid_len), F32),
            pltpu.VMEM((2, grid_len * (2 * k1_count + 1), grid_len), F32),
            pltpu.VMEM((grid_len * (k1_count + 1), grid_len), F32),
            pltpu.VMEM((3, piece * (box_edge + 1), lanes), F32),
            pltpu.VMEM((2 * box_edge, 2 * k1_count), BF16),
            pltpu.VMEM((2, 2 * box_edge, 2 * k1_count), BF16),
            pltpu.VMEM((2 * grid_len, lanes), BF16),
            pltpu.VMEM((2, 2 * grid_len, lanes), BF16),
        ] + [dma((sent,))] * 2 + [dma((numbers,))] * 6 + [
            pltpu.VMEM((numbers,) + flat, F32),
            pltpu.VMEM((numbers, 2) + flat, F32),
            pltpu.VMEM((numbers, 3) + flat, BF16),
            pltpu.VMEM((numbers, 3) + flat, BF16),
        ] + [pltpu.VMEM((numbers,) + flat, BF16)] * 4 + [pltpu.VMEM((sent,) + flat, BF16)] * 2,
        compiler_params=pltpu.CompilerParams(
            collective_id=1, has_side_effects=True, vmem_limit_bytes=60 * 1024 * 1024
        ),
        name="pair_terms",
    )(partners, boxes, kernel.reshape(grid_len * k1_count, grid_len), *tables)


def per_device(orbitals, partners, offsets, kernel):
    boxes = gather_boxes(orbitals, partners, offsets)
    return pair_terms(boxes, partners, kernel)[None]


def solution(mesh):
    return jax.shard_map(
        per_device,
        mesh=mesh,
        in_specs=(P("orb", "slab", None), P("orb", None), P("orb", None), P(None, "slab", None)),
        out_specs=P("orb", "slab", None),
        check_vma=False,
    )
```

```python
import functools
import math

import jax
import jax.numpy as jnp
import ml_dtypes
import numpy as np
from jax import lax
from jax.experimental import pallas as pl
from jax.experimental.pallas import tpu as pltpu
from jax.sharding import PartitionSpec as P

REACH = 4
F32 = jnp.float32
BF16 = jnp.bfloat16


def phases(places, frequency, grid_len, signed):
    wrapped = (places[:, None] * frequency[None, :]) % grid_len
    angles = wrapped.astype(np.float64) * (2.0 * math.pi / grid_len)
    return np.cos(angles), signed * np.sin(angles)


def block_form(cos, sin):
    return np.block([[cos, -sin], [sin, cos]])


def make_tables(box_edge, slab_count):
    grid_len = 2 * box_edge
    half = box_edge // 2
    k1_count = grid_len // slab_count
    box = np.arange(box_edge) + half
    grid = np.arange(grid_len)
    cos, sin = phases(box, grid, grid_len, -1.0)
    f2 = np.zeros((2 * box_edge, 2 * grid_len))
    f2[:box_edge] = np.concatenate([cos, sin], 1)
    f0 = block_form(cos.T, sin.T)
    f1 = []
    e1 = []
    gcos, gsin = phases(grid, grid, grid_len, 1.0)
    for s in range(slab_count):
        mine = slice(s * k1_count, (s + 1) * k1_count)
        f1.append(block_form(cos.T[mine], sin.T[mine]))
        e1.append(block_form(gcos[:, mine], gsin[:, mine]))
    e0 = block_form(gcos, gsin)
    e2 = np.concatenate([gcos.T, -gsin.T], 0) / grid_len**3
    tables = [f2, np.stack(f1), f0, e0, np.stack(e1), e2]
    return [t.astype(np.float32).astype(ml_dtypes.bfloat16) for t in tables]


def dot(a, b):
    return jnp.dot(a, b, preferred_element_type=F32)


def neighbours(orb_count):
    i = lax.axis_index("orb")
    core, side = lax.rem(i, 2), lax.rem(i // 2, 2)
    sibling = i + 1 - 2 * core
    across = i + 2 - 4 * side
    behind = lax.rem(i + orb_count - REACH, orb_count)
    ahead = lax.rem(i + REACH, orb_count)
    return i, core, side, sibling, across, behind, ahead


def slot_of(partner, i, side, orb_count):
    hop = jnp.minimum(lax.rem(partner - i + orb_count, orb_count), REACH)
    target = lax.rem(i, REACH) + hop
    group, place = target // REACH, lax.rem(target, REACH)
    return 2 * jnp.where(place // 2 == side, group, 2) + lax.rem(place, 2)


def remote(src, dst, send_sem, recv_sem, orb, slab):
    return pltpu.make_async_remote_copy(
        src_ref=src, dst_ref=dst, send_sem=send_sem, recv_sem=recv_sem,
        device_id=(orb, slab), device_id_type=pl.DeviceIdType.MESH,
    )


def greet(peers):
    barrier = pltpu.get_barrier_semaphore()
    for peer in peers:
        pl.semaphore_signal(barrier, inc=1, device_id=peer, device_id_type=pl.DeviceIdType.MESH)
    pl.semaphore_wait(barrier, len(peers))


def gather_kernel(
    orb_count, slab_count, chunks,
    partners_ref, offsets_ref, orbital_ref, out_ref,
    x_send, x_recv, z_send, z_recv, y_send, y_recv, core_send, core_recv,
    *held,
):
    i, core, side, sibling, across, behind, ahead = neighbours(orb_count)
    s = lax.axis_index("slab")
    others = [lax.rem(s + k, slab_count) for k in range(slab_count)]
    rows, cells = orbital_ref.shape
    width = out_ref.shape[3] // chunks
    cols = [pl.ds(q * width, width) for q in range(chunks)]

    lane = lax.broadcasted_iota(jnp.int32, (rows, 128), 1)
    corner = jnp.zeros((rows, 128), F32)
    for c in range(3):
        corner = jnp.where(lane == c, offsets_ref[0, c].astype(F32), corner)
    out_ref[s, 0, :, pl.ds(0, cells)] = orbital_ref[...]
    out_ref[s, 0, :, pl.ds(cells, 128)] = corner.astype(BF16)
    for q in range(chunks):
        held[q][core] = out_ref[s, 0, :, cols[q]]
    greet([(p, s) for p in (sibling, across, behind, ahead)] + [(i, o) for o in others[1:]])

    units = slab_count * chunks

    def along(u, source, target, send, recv, to):
        return remote(held[u].at[source], held[u].at[target], send, recv, to, s)

    x = [
        remote(held[q].at[core], held[(slab_count - k) * chunks + q].at[core], x_send.at[k, q], x_recv.at[k, q], i, others[k])
        for k in range(1, slab_count)
        for q in range(chunks)
    ]
    x_came = [
        remote(held[q].at[core], held[k * chunks + q].at[core], x_send.at[slab_count - k, q], x_recv.at[slab_count - k, q], i, others[k])
        for k in range(1, slab_count)
        for q in range(chunks)
    ]
    z = [along(u, core, 2 + core, z_send.at[u], z_recv.at[u], behind) for u in range(units)]
    y_here = [along(u, core, 4 + core, y_send.at[u], y_recv.at[u], across) for u in range(units)]
    y_pass = [along(u, 2 + core, 4 + core, y_send.at[u], y_recv.at[u], across) for u in range(units)]
    by_core = [
        [along(u, 2 * g + core, 2 * g + core, core_send.at[g, u], core_recv.at[g, u], sibling) for u in range(units)]
        for g in range(3)
    ]
    slots = [slot_of(partners_ref[0, n], i, side, orb_count) for n in range(2)]

    def send_own(u):
        if u >= chunks:
            x_came[u - chunks].wait_recv()
        z[u].start()
        pl.when(side == 1)(y_here[u].start)
        by_core[0][u].start()
        if u >= chunks:
            out_ref[others[u // chunks], 0, :, cols[u % chunks]] = held[u][core]

    def pass_on(u):
        z[u].wait_recv()
        pl.when(side == 0)(y_pass[u].start)
        by_core[1][u].start()

    def pass_last(u):
        y_here[u].wait_recv()
        by_core[2][u].start()

    def pick(u):
        for g in range(3):
            by_core[g][u].wait_recv()
        for n in range(2):
            out_ref[others[u // chunks], 1 + n, :, cols[u % chunks]] = held[u][slots[n]]

    for copy in x:
        copy.start()
    stages = [(send_own, 0), (pass_on, chunks), (pass_last, chunks + 1), (pick, chunks + 2)]
    for step in range(units + chunks + 2):
        for stage, lag in stages:
            if 0 <= step - lag < units:
                stage(step - lag)
    for copy in x + z + y_here + by_core[0] + by_core[1] + by_core[2]:
        copy.wait_send()


def gather_boxes(orbitals, partners, offsets):
    orb_count, slab_count = lax.axis_size("orb"), lax.axis_size("slab")
    rows, cells = orbitals.shape[1:]
    lanes = cells + 128
    chunks = 3 if lanes % (3 * 128) == 0 else 1
    smem = pl.BlockSpec(memory_space=pltpu.SMEM)
    vmem = pl.BlockSpec(memory_space=pltpu.VMEM)
    dma = pltpu.SemaphoreType.DMA
    units = slab_count * chunks
    return pl.pallas_call(
        functools.partial(gather_kernel, orb_count, slab_count, chunks),
        out_shape=jax.ShapeDtypeStruct((slab_count, 3, rows, lanes), BF16),
        in_specs=[smem, smem, vmem],
        out_specs=vmem,
        scratch_shapes=[
            dma((slab_count, chunks)), dma((slab_count, chunks)), dma((units,)), dma((units,)), dma((units,)), dma((units,)),
            dma((3, units)), dma((3, units)),
        ] + [pltpu.VMEM((6, rows, lanes // chunks), BF16)] * units,
        compiler_params=pltpu.CompilerParams(
            collective_id=0, has_side_effects=True, vmem_limit_bytes=32 * 1024 * 1024
        ),
        name="gather_boxes",
    )(partners, offsets, orbitals.reshape(rows, cells))


def pair_kernel(
    orb_count, box_edge, k1_count,
    partners_ref, boxes_ref, kernel_in, f2_in, f1_in, f0_in, e0_in, e1_in, e2_in,
    out_ref,
    kernel_ref, f2_ref, f1_ref, f0_ref, e0_ref, e1_ref, e2_ref, in_sem,
    cells, here, y_parts, v_parts, k_rows, terms, e1_own, e1_far, e2_own, e2_far,
    x_send, x_recv, core_send, core_recv, y_send, y_recv, z_send, z_recv,
    own_terms, kept, to_core, from_core, to_y, from_y, to_z, from_z, to_x, from_x,
):
    edge = box_edge
    grid_len = 2 * edge
    half = edge // 2
    lanes = 2 * edge
    slab_count, _, rows, _ = boxes_ref.shape
    i, core, side, sibling, across, behind, ahead = neighbours(orb_count)
    slab = lax.axis_index("slab")
    others = [lax.rem(slab + k, slab_count) for k in range(1, slab_count)]
    arrays_in = [kernel_in, f2_in, f1_in, f0_in, e0_in, e1_in, e2_in]
    arrays = [kernel_ref, f2_ref, f1_ref, f0_ref, e0_ref, e1_ref, e2_ref]
    loads = [pltpu.make_async_copy(a, b, in_sem.at[k]) for k, (a, b) in enumerate(zip(arrays_in, arrays))]
    for k in (6, 5, 1, 2, 0, 3, 4):
        loads[k].start()
    greet([(p, slab) for p in (sibling, across, behind, ahead)] + [(i, o) for o in others])

    lane = lax.broadcasted_iota(jnp.int32, (edge, lanes), 1)
    low_lanes = lane < edge
    row = lax.broadcasted_iota(jnp.int32, (edge, lanes), 0)
    corner_lane = lax.broadcasted_iota(jnp.int32, (1, lanes), 1)

    def corner(b):
        held = boxes_ref[0, b, :, pl.ds(edge * edge, lanes)].astype(F32)[0:1]
        return [jnp.sum(jnp.where(corner_lane == c, held, 0.0)).astype(jnp.int32) for c in range(3)]

    corners = [corner(b) for b in range(3)]
    shifts = [[jnp.clip(corners[1 + n][c] - corners[0][c], -half, half) for c in range(3)] for n in range(2)]
    cell_pitch = edge + half + 1
    term_pitch = edge + 1
    y_pitch = 2 * edge + 1
    v_pitch = 2 * k1_count + 1
    k_pitch = k1_count + 1

    no_rows = jnp.zeros((half + 8, lanes), F32)
    for b in range(3):
        cells[b, pl.ds(0, half), :] = jnp.zeros((half, lanes), F32)

    def clear(c0, carry):
        for b in range(3):
            cells[b, pl.ds(c0 * cell_pitch + cell_pitch - 1, half + 8), :] = no_rows
        return carry

    lax.fori_loop(0, edge, clear, 0, unroll=4)
    for b in range(3):
        cells[b, pl.ds(edge * cell_pitch, edge + 2 * half), :] = jnp.zeros((edge + 2 * half, lanes), F32)

    def unpack(g, carry):
        lo_at = pl.ds(half + 2 * g, edge, stride=cell_pitch)
        hi_at = pl.ds(half + 2 * g + 1, edge, stride=cell_pitch)
        for b in range(3):
            both = boxes_ref[:, b, :, pl.ds(pl.multiple_of(g * lanes, lanes), lanes)].astype(F32)
            both = both.reshape(edge, lanes)
            cells[b, lo_at, :] = jnp.where(low_lanes, both, 0.0)
            cells[b, hi_at, :] = jnp.where(low_lanes, pltpu.roll(both, edge, 1), 0.0)
        return carry

    lax.fori_loop(0, edge // 2, unpack, 0, unroll=4)

    for load in loads:
        load.wait()

    def spread(g, carry):
        for k in range(4):
            k0 = 4 * g + k
            k_rows[pl.ds(k0 * k_pitch, k1_count), :] = kernel_ref[pl.ds(pl.multiple_of(k0 * k1_count, k1_count), k1_count), :]
        return carry

    lax.fori_loop(0, edge // 2, spread, 0, unroll=2)

    e1_grid = e1_ref[slab]
    e2_grid = e2_ref[...]
    sel_lane = lax.broadcasted_iota(jnp.int32, (grid_len, lanes), 1)
    sel_row = lax.broadcasted_iota(jnp.int32, (grid_len, lanes), 0)

    def windows(d1, d2):
        pick_rows = (row + half + d1 == lane).astype(F32).astype(BF16)
        top = dot(pick_rows, e1_grid[:grid_len]).astype(BF16)
        bottom = dot(pick_rows, e1_grid[grid_len:]).astype(BF16)
        pick_cols = ((sel_lane + half + d2 == sel_row) & (sel_lane < edge)).astype(F32).astype(BF16)
        return jnp.concatenate([top, bottom], 0), dot(e2_grid, pick_cols).astype(BF16)

    e1_own[...], e2_own[...] = windows(0, 0)
    for n in range(2):
        e1_far[n], e2_far[n] = windows(shifts[n][1], shifts[n][2])

    def moved(b, c0, d0, d1, d2):
        source = c0 + d0
        at = jnp.where((source >= 0) & (source < edge), source, edge)
        block = cells[b, pl.ds(at * cell_pitch + half + d1, edge), :]
        return pltpu.roll(block, (-d2) & (lanes - 1), 1)

    batch = 4

    def forward(step, carry):
        z = []
        for j in range(batch):
            c0 = step * batch + j
            own = cells[0, pl.ds(c0 * cell_pitch + half, edge), :]
            for n in range(2):
                d0, d1, d2 = shifts[n]
                partner = moved(1 + n, c0, -d0, -d1, -d2)
                here[n, pl.ds(pl.multiple_of(c0 * edge, edge), edge), :] = partner
                z.append((own * partner).astype(BF16))
        z = dot(jnp.concatenate(z, 0), f2_ref[...]).astype(BF16)
        for j in range(batch):
            c0 = step * batch + j
            mine = [z[(2 * j + n) * edge : (2 * j + n + 1) * edge] for n in range(2)]
            mine = jnp.concatenate(
                [jnp.concatenate([m[:, :grid_len], m[:, grid_len:]], 0) for m in mine], 1
            )
            y = dot(f1_ref[slab], mine)
            for n in range(2):
                part = y[:, n * grid_len : (n + 1) * grid_len]
                y_parts[n, pl.ds(c0, k1_count, stride=y_pitch), :] = part[:k1_count]
                y_parts[n, pl.ds(edge + c0, k1_count, stride=y_pitch), :] = part[k1_count:]
        return carry

    lax.fori_loop(0, edge // batch, forward, 0, unroll=2)

    def middle(k1, carry):
        at = pl.ds(k1 * y_pitch, 2 * edge)
        y = jnp.concatenate([y_parts[n, at, :].astype(BF16) for n in range(2)], 1)
        x = dot(f0_ref[...], y)
        k = k_rows[pl.ds(k1, grid_len, stride=k_pitch), :]
        k = jnp.concatenate([k, k], 1)
        w = jnp.concatenate([(x[:grid_len] * k).astype(BF16), (x[grid_len:] * k).astype(BF16)], 0)
        v = dot(e0_ref[...], w)
        for n in range(2):
            part = v[:, n * grid_len : (n + 1) * grid_len]
            v_parts[n, pl.ds(k1, grid_len, stride=v_pitch), :] = part[:grid_len]
            v_parts[n, pl.ds(k1_count + k1, grid_len, stride=v_pitch), :] = part[grid_len:]
        return carry

    lax.fori_loop(0, k1_count, middle, 0, unroll=8)

    def v_rows(n, u0):
        u0 = jnp.clip(u0, 0, grid_len - 1)
        return v_parts[n, pl.ds(u0 * v_pitch, 2 * k1_count), :].astype(BF16)

    piece = own_terms.shape[1]
    pieces = rows // piece
    numbers = slab_count * pieces
    away = numbers - pieces
    slots = [slot_of(partners_ref[0, n], i, side, orb_count) for n in range(2)]

    parts = 4
    width = edge * edge // parts
    cols = [pl.ds(h * width, width) for h in range(parts)]

    def over_core(t, h):
        return remote(
            to_core.at[t, :, :, cols[h]], from_core.at[t, :, :, cols[h]], core_send.at[t, h], core_recv.at[t, h], sibling, slab
        )

    def over_y(t, h):
        return remote(to_y.at[t, :, cols[h]], from_y.at[t, :, cols[h]], y_send.at[t, h], y_recv.at[t, h], across, slab)

    def over_z(t, h):
        return remote(to_z.at[t, :, cols[h]], from_z.at[t, :, cols[h]], z_send.at[t, h], z_recv.at[t, h], ahead, slab)

    def over_x(t):
        target = lax.rem(slab + 1 + t // pieces, slab_count)
        return remote(to_x.at[t], from_x.at[t], x_send.at[t], x_recv.at[t], i, target)

    def compute(number):
        target = lax.rem(slab + 1 + number // pieces, slab_count)
        first = target * rows + lax.rem(number, pieces) * piece

        def backward(step, inner):
            u = []
            for j in range(batch):
                c0 = first + step * batch + j
                v = jnp.concatenate([v_rows(n, half + c0) for n in range(2)], 1)
                part = dot(e1_own[...], v).astype(BF16)
                for n in range(2):
                    mine = part[:, n * grid_len : (n + 1) * grid_len]
                    u.append(jnp.concatenate([mine[:edge], mine[edge:]], 1))
            field = dot(jnp.concatenate(u, 0), e2_own[...])
            for j in range(batch):
                c0 = first + step * batch + j
                at = pl.ds(pl.multiple_of(c0 * edge, edge), edge)
                own = field[2 * j * edge : (2 * j + 1) * edge] * here[0, at, :]
                own += field[(2 * j + 1) * edge : (2 * j + 2) * edge] * here[1, at, :]
                terms[0, pl.ds((step * batch + j) * term_pitch, edge), :] = own
            for n in range(2):
                d0, d1, d2 = shifts[n]
                u = []
                for j in range(batch):
                    mine = dot(e1_far[n], v_rows(n, half + d0 + first + step * batch + j)).astype(BF16)
                    u.append(jnp.concatenate([mine[:edge], mine[edge:]], 1))
                field = dot(jnp.concatenate(u, 0), e2_far[n])
                for j in range(batch):
                    there = moved(0, first + step * batch + j, d0, d1, d2)
                    to = pl.ds((step * batch + j) * term_pitch, edge)
                    terms[1 + n, to, :] = field[j * edge : (j + 1) * edge] * there
            return inner

        lax.fori_loop(0, piece // batch, backward, 0, unroll=2)

        def pack(g, inner):
            at = pl.ds(pl.multiple_of(g * lanes, lanes), lanes)
            both = []
            for b in range(3):
                lo = terms[b, pl.ds(2 * g, piece, stride=term_pitch), :]
                hi = terms[b, pl.ds(2 * g + 1, piece, stride=term_pitch), :]
                both.append(lo + pltpu.roll(hi, edge, 1))
            own_terms[number, :, at] = both[0]

            def share(slot):
                return jnp.where(slots[0] == slot, both[1], jnp.where(slots[1] == slot, both[2], 0.0))

            for group in range(3):
                to_core[number, group, :, at] = share(2 * group + 1 - core).astype(BF16)
            for group in range(1, 3):
                kept[number, group - 1, :, at] = share(2 * group + core)
            return inner

        for h in range(parts):
            share_of = edge // 2 // parts
            lax.fori_loop(h * share_of, (h + 1) * share_of, pack, 0, unroll=4)
            over_core(number, h).start()

    def after_core(t):
        for h in range(parts):
            over_core(t, h).wait_recv()
            at = cols[h]
            to_y[t, :, at] = (kept[t, 1, :, at] + from_core[t, 2, :, at].astype(F32)).astype(BF16)
            over_y(t, h).start()
            own_terms[t, :, at] += from_core[t, 0, :, at].astype(F32)
            kept[t, 0, :, at] += from_core[t, 1, :, at].astype(F32)

    def after_y(t):
        for h in range(parts):
            over_y(t, h).wait_recv()
            at = cols[h]
            came = from_y[t, :, at].astype(F32)
            to_z[t, :, at] = (kept[t, 0, :, at] + jnp.where(side == 0, came, 0.0)).astype(BF16)
            over_z(t, h).start()
            own_terms[t, :, at] += jnp.where(side == 1, came, 0.0)

    def after_z(t):
        for h in range(parts):
            over_z(t, h).wait_recv()
            own_terms[t, :, cols[h]] += from_z[t, :, cols[h]].astype(F32)

        @pl.when(t < away)
        def _():
            to_x[t] = own_terms[t].astype(BF16)
            over_x(t).start()

    def one_step(step, carry):
        for stage, lag in ((after_core, 1), (after_y, 2), (after_z, 3), (compute, 0)):
            pl.when((step >= lag) & (step < numbers + lag))(functools.partial(stage, step - lag))
        return carry

    lax.fori_loop(0, numbers + 3, one_step, 0)

    for q in range(pieces):
        total = own_terms[away + q]
        for k in range(slab_count - 1):
            over_x(k * pieces + q).wait_recv()
            total += from_x[k * pieces + q].astype(F32)
        out_ref[pl.ds(q * piece, piece), :] = total
    for t in range(numbers):
        for h in range(parts):
            over_core(t, h).wait_send()
            over_y(t, h).wait_send()
            over_z(t, h).wait_send()
        if t < away:
            over_x(t).wait_send()


def pair_terms(boxes, partners, kernel):
    orb_count = lax.axis_size("orb")
    slab_count, _, rows, _ = boxes.shape
    box_edge = slab_count * rows
    grid_len, k1_count = kernel.shape[0], kernel.shape[1]
    tables = make_tables(box_edge, slab_count)
    smem = pl.BlockSpec(memory_space=pltpu.SMEM)
    vmem = pl.BlockSpec(memory_space=pltpu.VMEM)
    cells = box_edge * box_edge
    cell_rows = (box_edge + 1) * (box_edge + box_edge // 2 + 1) + box_edge // 2 - 1
    arrays = [kernel.reshape(grid_len * k1_count, grid_len)] + tables
    lanes = 2 * box_edge
    piece = min(rows, 16)
    pieces = rows // piece
    numbers = slab_count * pieces
    sent = numbers - pieces
    flat = (piece, cells)
    dma = pltpu.SemaphoreType.DMA
    return pl.pallas_call(
        functools.partial(pair_kernel, orb_count, box_edge, k1_count),
        out_shape=jax.ShapeDtypeStruct((rows, cells), F32),
        in_specs=[smem, vmem] + [pl.BlockSpec(memory_space=pl.ANY)] * 7,
        out_specs=vmem,
        scratch_shapes=[pltpu.VMEM(a.shape, a.dtype) for a in arrays] + [
            dma((len(arrays),)),
            pltpu.VMEM((3, cell_rows, lanes), F32),
            pltpu.VMEM((2, cells, lanes), F32),
            pltpu.VMEM((2, k1_count * (2 * box_edge + 1), grid_len), F32),
            pltpu.VMEM((2, grid_len * (2 * k1_count + 1), grid_len), F32),
            pltpu.VMEM((grid_len * (k1_count + 1), grid_len), F32),
            pltpu.VMEM((3, piece * (box_edge + 1), lanes), F32),
            pltpu.VMEM((2 * box_edge, 2 * k1_count), BF16),
            pltpu.VMEM((2, 2 * box_edge, 2 * k1_count), BF16),
            pltpu.VMEM((2 * grid_len, lanes), BF16),
            pltpu.VMEM((2, 2 * grid_len, lanes), BF16),
        ] + [dma((sent,))] * 2 + [dma((numbers, 4))] * 6 + [
            pltpu.VMEM((numbers,) + flat, F32),
            pltpu.VMEM((numbers, 2) + flat, F32),
            pltpu.VMEM((numbers, 3) + flat, BF16),
            pltpu.VMEM((numbers, 3) + flat, BF16),
        ] + [pltpu.VMEM((numbers,) + flat, BF16)] * 4 + [pltpu.VMEM((sent,) + flat, BF16)] * 2,
        compiler_params=pltpu.CompilerParams(
            collective_id=1, has_side_effects=True, vmem_limit_bytes=60 * 1024 * 1024
        ),
        name="pair_terms",
    )(partners, boxes, *arrays)


def per_device(orbitals, partners, offsets, kernel):
    boxes = gather_boxes(orbitals, partners, offsets)
    return pair_terms(boxes, partners, kernel)[None]


def solution(mesh):
    return jax.shard_map(
        per_device,
        mesh=mesh,
        in_specs=(P("orb", "slab", None), P("orb", None), P("orb", None), P(None, "slab", None)),
        out_specs=P("orb", "slab", None),
        check_vma=False,
    )
```

```python
import functools
import math

import jax
import jax.numpy as jnp
import ml_dtypes
import numpy as np
from jax import lax
from jax.experimental import pallas as pl
from jax.experimental.pallas import tpu as pltpu
from jax.sharding import PartitionSpec as P

REACH = 4
F32 = jnp.float32
BF16 = jnp.bfloat16


def phases(places, frequency, grid_len, signed):
    wrapped = (places[:, None] * frequency[None, :]) % grid_len
    angles = wrapped.astype(np.float64) * (2.0 * math.pi / grid_len)
    return np.cos(angles), signed * np.sin(angles)


def block_form(cos, sin):
    return np.block([[cos, -sin], [sin, cos]])


def halves(table):
    return np.stack(np.split(table, 2, axis=1))


def make_tables(box_edge, slab_count):
    grid_len = 2 * box_edge
    half = box_edge // 2
    k1_count = grid_len // slab_count
    box = np.arange(box_edge) + half
    grid = np.arange(grid_len)
    cos, sin = phases(box, grid, grid_len, -1.0)
    f2 = np.zeros((2 * box_edge, 2 * grid_len))
    f2[:box_edge] = np.concatenate([cos, sin], 1)
    f0 = block_form(cos.T, sin.T)
    f1 = []
    e1 = []
    gcos, gsin = phases(grid, grid, grid_len, 1.0)
    for s in range(slab_count):
        mine = slice(s * k1_count, (s + 1) * k1_count)
        f1.append(block_form(cos.T[mine], sin.T[mine]))
        e1.append(block_form(gcos[:, mine], gsin[:, mine]))
    e0 = block_form(gcos, gsin)
    e2 = np.concatenate([gcos.T, -gsin.T], 0) / grid_len**3
    tables = [halves(f2), np.stack(f1), f0, halves(e0), np.stack(e1), e2]
    return [t.astype(np.float32).astype(ml_dtypes.bfloat16) for t in tables]


def dot(a, b):
    return jnp.dot(a, b, preferred_element_type=F32)


def neighbours(orb_count):
    i = lax.axis_index("orb")
    core, side = lax.rem(i, 2), lax.rem(i // 2, 2)
    sibling = i + 1 - 2 * core
    across = i + 2 - 4 * side
    behind = lax.rem(i + orb_count - REACH, orb_count)
    ahead = lax.rem(i + REACH, orb_count)
    return i, core, side, sibling, across, behind, ahead


def slot_of(partner, i, side, orb_count):
    hop = jnp.minimum(lax.rem(partner - i + orb_count, orb_count), REACH)
    target = lax.rem(i, REACH) + hop
    group, place = target // REACH, lax.rem(target, REACH)
    return 2 * jnp.where(place // 2 == side, group, 2) + lax.rem(place, 2)


def remote(src, dst, send_sem, recv_sem, orb, slab):
    return pltpu.make_async_remote_copy(
        src_ref=src, dst_ref=dst, send_sem=send_sem, recv_sem=recv_sem,
        device_id=(orb, slab), device_id_type=pl.DeviceIdType.MESH,
    )


def greet(peers):
    barrier = pltpu.get_barrier_semaphore()
    for peer in peers:
        pl.semaphore_signal(barrier, inc=1, device_id=peer, device_id_type=pl.DeviceIdType.MESH)
    pl.semaphore_wait(barrier, len(peers))


def pair_kernel(
    orb_count, slab_count, box_edge, k1_count, chunks,
    partners_ref, offsets_ref, orbital_ref, kernel_in, f2_in, f1_in, f0_in, e0_in, e1_in, e2_in,
    out_ref,
    f2_ref, f1_ref, f0_ref, e0_ref, e1_ref, e2_ref, in_sem,
    own_send, own_recv, ahead_send, ahead_recv, side_send, side_recv, sib_send, sib_recv,
    cells, here, y_parts, v_parts, k_rows, terms, e1_own, e1_far, e2_own, e2_far,
    x_send, x_recv, core_send, core_recv, y_send, y_recv, z_send, z_recv,
    own_terms, kept, to_core, from_core, to_y, from_y, to_z, from_z, to_x, from_x,
    *held,
):
    edge = box_edge
    grid_len = 2 * edge
    half = edge // 2
    lanes = 2 * edge
    rows, cell_count = orbital_ref.shape
    i, core, side, sibling, across, behind, ahead = neighbours(orb_count)
    slab = lax.axis_index("slab")
    others = [lax.rem(slab + k, slab_count) for k in range(slab_count)]
    kernel_ref = v_parts.at[0, pl.ds(0, grid_len * k1_count), :]
    arrays_in = [kernel_in, f2_in, f1_in, f0_in, e0_in, e1_in, e2_in]
    arrays = [kernel_ref, f2_ref, f1_ref, f0_ref, e0_ref, e1_ref, e2_ref]
    loads = [pltpu.make_async_copy(a, b, in_sem.at[k]) for k, (a, b) in enumerate(zip(arrays_in, arrays))]
    for k in (6, 5, 1, 2, 0, 3, 4):
        loads[k].start()

    per_chunk = (cell_count + lanes) // (lanes * chunks)
    width = per_chunk * lanes
    units = slab_count * chunks
    corner_at = (per_chunk - 1) * lanes
    lane = lax.broadcasted_iota(jnp.int32, (rows, lanes), 1)
    low_half = lane < edge
    own_corner = jnp.zeros((rows, lanes), F32)
    for c in range(3):
        own_corner = jnp.where(lane == c, offsets_ref[0, c].astype(F32), own_corner)
    for q in range(chunks):
        size = width if q < chunks - 1 else width - lanes
        held[q][core, :, pl.ds(0, size)] = orbital_ref[:, pl.ds(q * width, size)]
    held[chunks - 1][core, :, pl.ds(corner_at, lanes)] = own_corner.astype(BF16)
    greet([(p, slab) for p in (sibling, across, behind, ahead)] + [(i, o) for o in others[1:]])

    def along(u, source, target, send, recv, to):
        return remote(held[u].at[source], held[u].at[target], send, recv, to, slab)

    def to_slab(k, q):
        back = slab_count - k
        return remote(held[q].at[core], held[back * chunks + q].at[core], own_send.at[k, q], own_recv.at[k, q], i, others[k])

    def from_slab(k, q):
        back = slab_count - k
        return remote(held[q].at[core], held[k * chunks + q].at[core], own_send.at[back, q], own_recv.at[back, q], i, others[k])

    x_sends = [to_slab(k, q) for k in range(1, slab_count) for q in range(chunks)]
    x_comes = [from_slab(k, q) for k in range(1, slab_count) for q in range(chunks)]
    z_boxes = [along(u, core, 2 + core, ahead_send.at[u], ahead_recv.at[u], behind) for u in range(units)]
    y_here = [along(u, core, 4 + core, side_send.at[u], side_recv.at[u], across) for u in range(units)]
    y_pass = [along(u, 2 + core, 4 + core, side_send.at[u], side_recv.at[u], across) for u in range(units)]
    by_core = [
        [along(u, 2 * g + core, 2 * g + core, sib_send.at[g, u], sib_recv.at[g, u], sibling) for u in range(units)]
        for g in range(3)
    ]
    slots = [slot_of(partners_ref[0, n], i, side, orb_count) for n in range(2)]
    cell_pitch = edge + half + 1
    term_pitch = edge + 1
    y_pitch = 2 * edge + 1
    v_pitch = 2 * k1_count + 1
    k_pitch = k1_count + 1

    no_rows = jnp.zeros((half + 8, lanes), F32)

    def clear(c0, carry):
        for b in range(3):
            cells[b, pl.ds(c0 * cell_pitch + cell_pitch - 1, half + 8), :] = no_rows
        return carry

    def clear_all():
        for b in range(3):
            cells[b, pl.ds(0, half), :] = jnp.zeros((half, lanes), F32)
        lax.fori_loop(0, edge, clear, 0, unroll=4)
        for b in range(3):
            cells[b, pl.ds(edge * cell_pitch, edge + 2 * half), :] = jnp.zeros((edge + 2 * half, lanes), F32)

    def unpack(u, b, slot):
        k, q = u // chunks, u % chunks
        base = others[k] * (rows * cell_pitch) + half + 2 * q * per_chunk

        def one(g, carry):
            both = held[u][slot, :, pl.ds(pl.multiple_of(g * lanes, lanes), lanes)].astype(F32)
            cells[b, pl.ds(base + 2 * g, rows, stride=cell_pitch), :] = jnp.where(low_half, both, 0.0)
            other = jnp.where(low_half, pltpu.roll(both, edge, 1), 0.0)
            cells[b, pl.ds(base + 2 * g + 1, rows, stride=cell_pitch), :] = other
            return carry

        lax.fori_loop(0, per_chunk - (q == chunks - 1), one, 0, unroll=True)

    def spread(g, carry):
        for k in range(4):
            k0 = 4 * g + k
            at = pl.ds(pl.multiple_of(k0 * k1_count, k1_count), k1_count)
            k_rows[pl.ds(k0 * k_pitch, k1_count), :] = v_parts[0, at, :]
        return carry

    def send_own(u):
        if u >= chunks:
            x_comes[u - chunks].wait_recv()
        z_boxes[u].start()
        pl.when(side == 1)(y_here[u].start)
        by_core[0][u].start()
        if u >= chunks:
            unpack(u, 0, core)

    def pass_on(u):
        z_boxes[u].wait_recv()
        pl.when(side == 0)(y_pass[u].start)
        by_core[1][u].start()

    def pass_last(u):
        y_here[u].wait_recv()
        by_core[2][u].start()

    def pick(u):
        for g in range(3):
            by_core[g][u].wait_recv()
        for n in range(2):
            unpack(u, 1 + n, slots[n])

    for copy in x_sends:
        copy.start()
    stages = [(send_own, 0), (pass_on, chunks), (pass_last, chunks + 1), (pick, chunks + 2)]
    for step in range(units + chunks + 2):
        if step == chunks:
            clear_all()
            for u in range(chunks):
                unpack(u, 0, core)
        for stage, lag in stages:
            if 0 <= step - lag < units:
                stage(step - lag)
        if step == chunks + 1:
            for load in loads:
                load.wait()
            lax.fori_loop(0, edge // 2, spread, 0, unroll=2)

    corner_lane = lax.broadcasted_iota(jnp.int32, (1, lanes), 1)

    def corner(n):
        came = held[chunks - 1][slots[n], :, pl.ds(corner_at, lanes)].astype(F32)[0:1]
        return [jnp.sum(jnp.where(corner_lane == c, came, 0.0)).astype(jnp.int32) for c in range(3)]

    corners = [corner(n) for n in range(2)]
    shifts = [[jnp.clip(corners[n][c] - offsets_ref[0, c], -half, half) for c in range(3)] for n in range(2)]

    row = lax.broadcasted_iota(jnp.int32, (edge, lanes), 0)
    box_lane = lax.broadcasted_iota(jnp.int32, (edge, lanes), 1)

    e1_grid = e1_ref[slab]
    e2_grid = e2_ref[...]
    sel_lane = lax.broadcasted_iota(jnp.int32, (grid_len, lanes), 1)
    sel_row = lax.broadcasted_iota(jnp.int32, (grid_len, lanes), 0)

    def windows(d1, d2):
        pick_rows = (row + half + d1 == box_lane).astype(F32).astype(BF16)
        top = dot(pick_rows, e1_grid[:grid_len]).astype(BF16)
        bottom = dot(pick_rows, e1_grid[grid_len:]).astype(BF16)
        pick_cols = ((sel_lane + half + d2 == sel_row) & (sel_lane < edge)).astype(F32).astype(BF16)
        return jnp.concatenate([top, bottom], 0), dot(e2_grid, pick_cols).astype(BF16)

    e1_own[...], e2_own[...] = windows(0, 0)
    for n in range(2):
        e1_far[n], e2_far[n] = windows(shifts[n][1], shifts[n][2])

    def moved(b, c0, d0, d1, d2):
        source = c0 + d0
        at = jnp.where((source >= 0) & (source < edge), source, edge)
        block = cells[b, pl.ds(at * cell_pitch + half + d1, edge), :]
        return pltpu.roll(block, (-d2) & (lanes - 1), 1)

    batch = 4

    def forward(step, carry):
        z = []
        for j in range(batch):
            c0 = step * batch + j
            own = cells[0, pl.ds(c0 * cell_pitch + half, edge), :]
            for n in range(2):
                d0, d1, d2 = shifts[n]
                partner = moved(1 + n, c0, -d0, -d1, -d2)
                here[n, pl.ds(pl.multiple_of(c0 * edge, edge), edge), :] = partner
                z.append((own * partner).astype(BF16))
        z = dot(jnp.concatenate(z, 0), jnp.concatenate([f2_ref[0], f2_ref[1]], 1)).astype(BF16)
        for j in range(batch):
            c0 = step * batch + j
            mine = [z[(2 * j + n) * edge : (2 * j + n + 1) * edge] for n in range(2)]
            mine = jnp.concatenate(
                [jnp.concatenate([m[:, :grid_len], m[:, grid_len:]], 0) for m in mine], 1
            )
            y = dot(f1_ref[slab], mine)
            for n in range(2):
                part = y[:, n * grid_len : (n + 1) * grid_len]
                y_parts[n, pl.ds(c0, k1_count, stride=y_pitch), :] = part[:k1_count]
                y_parts[n, pl.ds(edge + c0, k1_count, stride=y_pitch), :] = part[k1_count:]
        return carry

    lax.fori_loop(0, edge // batch, forward, 0, unroll=2)

    def middle(k1, carry):
        at = pl.ds(k1 * y_pitch, 2 * edge)
        y = jnp.concatenate([y_parts[n, at, :].astype(BF16) for n in range(2)], 1)
        x = dot(f0_ref[...], y)
        k = k_rows[pl.ds(k1, grid_len, stride=k_pitch), :]
        k = jnp.concatenate([k, k], 1)
        w = jnp.concatenate([(x[:grid_len] * k).astype(BF16), (x[grid_len:] * k).astype(BF16)], 0)
        v = dot(jnp.concatenate([e0_ref[0], e0_ref[1]], 1), w)
        for n in range(2):
            part = v[:, n * grid_len : (n + 1) * grid_len]
            v_parts[n, pl.ds(k1, grid_len, stride=v_pitch), :] = part[:grid_len]
            v_parts[n, pl.ds(k1_count + k1, grid_len, stride=v_pitch), :] = part[grid_len:]
        return carry

    lax.fori_loop(0, k1_count, middle, 0, unroll=8)

    def v_rows(n, u0):
        u0 = jnp.clip(u0, 0, grid_len - 1)
        return v_parts[n, pl.ds(u0 * v_pitch, 2 * k1_count), :].astype(BF16)

    piece = own_terms.shape[1]
    pieces = rows // piece
    numbers = slab_count * pieces
    away = numbers - pieces

    parts = 4
    part_width = edge * edge // parts
    cols = [pl.ds(h * part_width, part_width) for h in range(parts)]

    def over_core(t, h):
        return remote(
            to_core.at[t, :, :, cols[h]], from_core.at[t, :, :, cols[h]], core_send.at[t, h], core_recv.at[t, h], sibling, slab
        )

    def over_y(t, h):
        return remote(to_y.at[t, :, cols[h]], from_y.at[t, :, cols[h]], y_send.at[t, h], y_recv.at[t, h], across, slab)

    def over_z(t, h):
        return remote(to_z.at[t, :, cols[h]], from_z.at[t, :, cols[h]], z_send.at[t, h], z_recv.at[t, h], ahead, slab)

    def over_x(t):
        target = lax.rem(slab + 1 + t // pieces, slab_count)
        return remote(to_x.at[t], from_x.at[t], x_send.at[t], x_recv.at[t], i, target)

    def compute(number):
        target = lax.rem(slab + 1 + number // pieces, slab_count)
        first = target * rows + lax.rem(number, pieces) * piece

        def backward(step, inner):
            u = []
            for j in range(batch):
                c0 = first + step * batch + j
                v = jnp.concatenate([v_rows(n, half + c0) for n in range(2)], 1)
                part = dot(e1_own[...], v).astype(BF16)
                for n in range(2):
                    mine = part[:, n * grid_len : (n + 1) * grid_len]
                    u.append(jnp.concatenate([mine[:edge], mine[edge:]], 1))
            field = dot(jnp.concatenate(u, 0), e2_own[...])
            for j in range(batch):
                c0 = first + step * batch + j
                at = pl.ds(pl.multiple_of(c0 * edge, edge), edge)
                own = field[2 * j * edge : (2 * j + 1) * edge] * here[0, at, :]
                own += field[(2 * j + 1) * edge : (2 * j + 2) * edge] * here[1, at, :]
                terms[0, pl.ds((step * batch + j) * term_pitch, edge), :] = own
            for n in range(2):
                d0, d1, d2 = shifts[n]
                u = []
                for j in range(batch):
                    mine = dot(e1_far[n], v_rows(n, half + d0 + first + step * batch + j)).astype(BF16)
                    u.append(jnp.concatenate([mine[:edge], mine[edge:]], 1))
                field = dot(jnp.concatenate(u, 0), e2_far[n])
                for j in range(batch):
                    there = moved(0, first + step * batch + j, d0, d1, d2)
                    to = pl.ds((step * batch + j) * term_pitch, edge)
                    terms[1 + n, to, :] = field[j * edge : (j + 1) * edge] * there
            return inner

        lax.fori_loop(0, piece // batch, backward, 0, unroll=2)

        def pack(g, inner):
            at = pl.ds(pl.multiple_of(g * lanes, lanes), lanes)
            both = []
            for b in range(3):
                lo = terms[b, pl.ds(2 * g, piece, stride=term_pitch), :]
                hi = terms[b, pl.ds(2 * g + 1, piece, stride=term_pitch), :]
                both.append(lo + pltpu.roll(hi, edge, 1))
            own_terms[number, :, at] = both[0]

            def share(slot):
                return jnp.where(slots[0] == slot, both[1], jnp.where(slots[1] == slot, both[2], 0.0))

            for group in range(3):
                to_core[number, group, :, at] = share(2 * group + 1 - core).astype(BF16)
            for group in range(1, 3):
                kept[number, group - 1, :, at] = share(2 * group + core)
            return inner

        for h in range(parts):
            share_of = edge // 2 // parts
            lax.fori_loop(h * share_of, (h + 1) * share_of, pack, 0, unroll=4)
            over_core(number, h).start()

    def after_core(t):
        for h in range(parts):
            over_core(t, h).wait_recv()
            at = cols[h]
            to_y[t, :, at] = (kept[t, 1, :, at] + from_core[t, 2, :, at].astype(F32)).astype(BF16)
            over_y(t, h).start()
            own_terms[t, :, at] += from_core[t, 0, :, at].astype(F32)
            kept[t, 0, :, at] += from_core[t, 1, :, at].astype(F32)

    def after_y(t):
        for h in range(parts):
            over_y(t, h).wait_recv()
            at = cols[h]
            came = from_y[t, :, at].astype(F32)
            to_z[t, :, at] = (kept[t, 0, :, at] + jnp.where(side == 0, came, 0.0)).astype(BF16)
            over_z(t, h).start()
            own_terms[t, :, at] += jnp.where(side == 1, came, 0.0)

    def after_z(t):
        for h in range(parts):
            over_z(t, h).wait_recv()
            own_terms[t, :, cols[h]] += from_z[t, :, cols[h]].astype(F32)

        @pl.when(t < away)
        def _():
            to_x[t] = own_terms[t].astype(BF16)
            over_x(t).start()

    def one_step(step, carry):
        for stage, lag in ((after_core, 1), (after_y, 2), (after_z, 3), (compute, 0)):
            pl.when((step >= lag) & (step < numbers + lag))(functools.partial(stage, step - lag))
        return carry

    lax.fori_loop(0, numbers + 3, one_step, 0)

    for q in range(pieces):
        total = own_terms[away + q]
        for k in range(slab_count - 1):
            over_x(k * pieces + q).wait_recv()
            total += from_x[k * pieces + q].astype(F32)
        out_ref[pl.ds(q * piece, piece), :] = total
    for t in range(numbers):
        for h in range(parts):
            over_core(t, h).wait_send()
            over_y(t, h).wait_send()
            over_z(t, h).wait_send()
        if t < away:
            over_x(t).wait_send()
    for copy in x_sends + z_boxes + y_here + by_core[0] + by_core[1] + by_core[2]:
        copy.wait_send()


def pair_terms(orbitals, partners, offsets, kernel):
    orb_count = lax.axis_size("orb")
    slab_count = lax.axis_size("slab")
    rows, cells = orbitals.shape[1:]
    box_edge = slab_count * rows
    grid_len, k1_count = kernel.shape[0], kernel.shape[1]
    tables = make_tables(box_edge, slab_count)
    smem = pl.BlockSpec(memory_space=pltpu.SMEM)
    vmem = pl.BlockSpec(memory_space=pltpu.VMEM)
    chunks = 3 if (cells // 128 + 1) % 3 == 0 else 1
    units = slab_count * chunks
    cell_rows = (box_edge + 1) * (box_edge + box_edge // 2 + 1) + box_edge // 2 - 1
    arrays = [kernel.reshape(grid_len * k1_count, grid_len)] + tables
    lanes = 2 * box_edge
    piece = min(rows, 16)
    pieces = rows // piece
    numbers = slab_count * pieces
    sent = numbers - pieces
    flat = (piece, cells)
    dma = pltpu.SemaphoreType.DMA
    return pl.pallas_call(
        functools.partial(pair_kernel, orb_count, slab_count, box_edge, k1_count, chunks),
        out_shape=jax.ShapeDtypeStruct((rows, cells), F32),
        in_specs=[smem, smem, vmem] + [pl.BlockSpec(memory_space=pl.ANY)] * 7,
        out_specs=vmem,
        scratch_shapes=[pltpu.VMEM(a.shape, a.dtype) for a in tables] + [
            dma((len(arrays),)),
            dma((slab_count, chunks)), dma((slab_count, chunks)), dma((units,)), dma((units,)), dma((units,)), dma((units,)),
            dma((3, units)), dma((3, units)),
            pltpu.VMEM((3, cell_rows, lanes), F32),
            pltpu.VMEM((2, cells, lanes), F32),
            pltpu.VMEM((2, k1_count * (2 * box_edge + 1), grid_len), F32),
            pltpu.VMEM((2, grid_len * (2 * k1_count + 1), grid_len), F32),
            pltpu.VMEM((grid_len * (k1_count + 1), grid_len), F32),
            pltpu.VMEM((3, piece * (box_edge + 1), lanes), F32),
            pltpu.VMEM((2 * box_edge, 2 * k1_count), BF16),
            pltpu.VMEM((2, 2 * box_edge, 2 * k1_count), BF16),
            pltpu.VMEM((2 * grid_len, lanes), BF16),
            pltpu.VMEM((2, 2 * grid_len, lanes), BF16),
        ] + [dma((sent,))] * 2 + [dma((numbers, 4))] * 6 + [
            pltpu.VMEM((numbers,) + flat, F32),
            pltpu.VMEM((numbers, 2) + flat, F32),
            pltpu.VMEM((numbers, 3) + flat, BF16),
            pltpu.VMEM((numbers, 3) + flat, BF16),
        ] + [pltpu.VMEM((numbers,) + flat, BF16)] * 4 + [pltpu.VMEM((sent,) + flat, BF16)] * 2 + [
            pltpu.VMEM((6, rows, (cells + lanes) // chunks), BF16)
        ] * units,
        compiler_params=pltpu.CompilerParams(
            collective_id=0, has_side_effects=True, vmem_limit_bytes=60 * 1024 * 1024
        ),
        name="pair_terms",
    )(partners, offsets, orbitals.reshape(rows, cells), *arrays)


def per_device(orbitals, partners, offsets, kernel):
    return pair_terms(orbitals, partners, offsets, kernel)[None]


def solution(mesh):
    return jax.shard_map(
        per_device,
        mesh=mesh,
        in_specs=(P("orb", "slab", None), P("orb", None), P("orb", None), P(None, "slab", None)),
        out_specs=P("orb", "slab", None),
        check_vma=False,
    )
```

```python
import functools
import math

import jax
import jax.numpy as jnp
import ml_dtypes
import numpy as np
from jax import lax
from jax.experimental import pallas as pl
from jax.experimental.pallas import tpu as pltpu
from jax.sharding import PartitionSpec as P

REACH = 4
F32 = jnp.float32
BF16 = jnp.bfloat16


def phases(places, frequency, grid_len, signed):
    wrapped = (places[:, None] * frequency[None, :]) % grid_len
    angles = wrapped.astype(np.float64) * (2.0 * math.pi / grid_len)
    return np.cos(angles), signed * np.sin(angles)


def block_form(cos, sin):
    return np.block([[cos, -sin], [sin, cos]])


def halves(table):
    return np.stack(np.split(table, 2, axis=1))


def make_tables(box_edge, slab_count):
    grid_len = 2 * box_edge
    half = box_edge // 2
    k1_count = grid_len // slab_count
    box = np.arange(box_edge) + half
    grid = np.arange(grid_len)
    cos, sin = phases(box, grid, grid_len, -1.0)
    f2 = np.zeros((2 * box_edge, 2 * grid_len))
    f2[:box_edge] = np.concatenate([cos, sin], 1)
    f0 = block_form(cos.T, sin.T)
    f1 = []
    e1 = []
    gcos, gsin = phases(grid, grid, grid_len, 1.0)
    for s in range(slab_count):
        mine = slice(s * k1_count, (s + 1) * k1_count)
        f1.append(block_form(cos.T[mine], sin.T[mine]))
        e1.append(block_form(gcos[:, mine], gsin[:, mine]))
    e0 = block_form(gcos, gsin)
    e2 = np.concatenate([gcos.T, -gsin.T], 0) / grid_len**3
    tables = [halves(f2), np.stack(f1), f0, halves(e0), np.stack(e1), e2]
    return [t.astype(np.float32).astype(ml_dtypes.bfloat16) for t in tables]


def dot(a, b):
    return jnp.dot(a, b, preferred_element_type=F32)


def neighbours(orb_count):
    i = lax.axis_index("orb")
    core, side = lax.rem(i, 2), lax.rem(i // 2, 2)
    sibling = i + 1 - 2 * core
    across = i + 2 - 4 * side
    behind = lax.rem(i + orb_count - REACH, orb_count)
    ahead = lax.rem(i + REACH, orb_count)
    return i, core, side, sibling, across, behind, ahead


def slot_of(partner, i, side, orb_count):
    hop = jnp.minimum(lax.rem(partner - i + orb_count, orb_count), REACH)
    target = lax.rem(i, REACH) + hop
    group, place = target // REACH, lax.rem(target, REACH)
    return 2 * jnp.where(place // 2 == side, group, 2) + lax.rem(place, 2)


def remote(src, dst, send_sem, recv_sem, orb, slab):
    return pltpu.make_async_remote_copy(
        src_ref=src, dst_ref=dst, send_sem=send_sem, recv_sem=recv_sem,
        device_id=(orb, slab), device_id_type=pl.DeviceIdType.MESH,
    )


def greet(peers):
    barrier = pltpu.get_barrier_semaphore()
    for peer in peers:
        pl.semaphore_signal(barrier, inc=1, device_id=peer, device_id_type=pl.DeviceIdType.MESH)
    pl.semaphore_wait(barrier, len(peers))


def pair_kernel(
    orb_count, slab_count, box_edge, k1_count, chunks,
    partners_ref, offsets_ref, orbital_ref, kernel_in, f2_in, f1_in, f0_in, e0_in, e1_in, e2_in,
    out_ref,
    f2_ref, f1_ref, f0_ref, e0_ref, e1_ref, e2_ref, in_sem,
    own_send, own_recv, ahead_send, ahead_recv, side_send, side_recv, sib_send, sib_recv,
    cells, here, y_parts, v_parts, k_rows, terms, e1_own, e1_far, e2_own, e2_far,
    x_send, x_recv, core_send, core_recv, y_send, y_recv, z_send, z_recv,
    own_terms, kept, to_core, from_core, to_y, from_y, to_z, from_z, to_x, from_x,
    *held,
):
    edge = box_edge
    grid_len = 2 * edge
    half = edge // 2
    lanes = 2 * edge
    rows, cell_count = orbital_ref.shape
    i, core, side, sibling, across, behind, ahead = neighbours(orb_count)
    slab = lax.axis_index("slab")
    others = [lax.rem(slab + k, slab_count) for k in range(slab_count)]
    kernel_ref = v_parts.at[0, pl.ds(0, grid_len * k1_count), :]
    arrays_in = [kernel_in, f2_in, f1_in, f0_in, e0_in, e1_in, e2_in]
    arrays = [kernel_ref, f2_ref, f1_ref, f0_ref, e0_ref, e1_ref, e2_ref]
    loads = [pltpu.make_async_copy(a, b, in_sem.at[k]) for k, (a, b) in enumerate(zip(arrays_in, arrays))]
    for k in (6, 5, 1, 2, 0, 3, 4):
        loads[k].start()

    per_chunk = (cell_count + lanes) // (lanes * chunks)
    width = per_chunk * lanes
    units = slab_count * chunks
    corner_at = (per_chunk - 1) * lanes
    lane = lax.broadcasted_iota(jnp.int32, (rows, lanes), 1)
    low_half = lane < edge
    own_corner = jnp.zeros((rows, lanes), F32)
    for c in range(3):
        own_corner = jnp.where(lane == c, offsets_ref[0, c].astype(F32), own_corner)
    for q in range(chunks):
        size = width if q < chunks - 1 else width - lanes
        held[q][core, :, pl.ds(0, size)] = orbital_ref[:, pl.ds(q * width, size)]
    held[chunks - 1][core, :, pl.ds(corner_at, lanes)] = own_corner.astype(BF16)
    greet([(p, slab) for p in (sibling, across, behind, ahead)] + [(i, o) for o in others[1:]])

    def along(u, source, target, send, recv, to):
        return remote(held[u].at[source], held[u].at[target], send, recv, to, slab)

    def to_slab(k, q):
        back = slab_count - k
        return remote(held[q].at[core], held[back * chunks + q].at[core], own_send.at[k, q], own_recv.at[k, q], i, others[k])

    def from_slab(k, q):
        back = slab_count - k
        return remote(held[q].at[core], held[k * chunks + q].at[core], own_send.at[back, q], own_recv.at[back, q], i, others[k])

    x_sends = [to_slab(k, q) for k in range(1, slab_count) for q in range(chunks)]
    x_comes = [from_slab(k, q) for k in range(1, slab_count) for q in range(chunks)]
    z_boxes = [along(u, core, 2 + core, ahead_send.at[u], ahead_recv.at[u], behind) for u in range(units)]
    y_here = [along(u, core, 4 + core, side_send.at[u], side_recv.at[u], across) for u in range(units)]
    y_pass = [along(u, 2 + core, 4 + core, side_send.at[u], side_recv.at[u], across) for u in range(units)]
    by_core = [
        [along(u, 2 * g + core, 2 * g + core, sib_send.at[g, u], sib_recv.at[g, u], sibling) for u in range(units)]
        for g in range(3)
    ]
    slots = [slot_of(partners_ref[0, n], i, side, orb_count) for n in range(2)]
    cell_pitch = edge + half + 1
    term_pitch = edge + 1
    y_pitch = 2 * edge + 1
    v_pitch = 2 * k1_count + 1
    k_pitch = k1_count + 1

    no_rows = jnp.zeros((half + 8, lanes), F32)

    def clear(c0, carry):
        for b in range(3):
            cells[b, pl.ds(c0 * cell_pitch + cell_pitch - 1, half + 8), :] = no_rows
        return carry

    def clear_all():
        for b in range(3):
            cells[b, pl.ds(0, half), :] = jnp.zeros((half, lanes), F32)
        lax.fori_loop(0, edge, clear, 0, unroll=4)
        for b in range(3):
            cells[b, pl.ds(edge * cell_pitch, edge + 2 * half), :] = jnp.zeros((edge + 2 * half, lanes), F32)

    def unpack(u, b, slot):
        k, q = u // chunks, u % chunks
        base = others[k] * (rows * cell_pitch) + half + 2 * q * per_chunk

        def one(g, carry):
            both = held[u][slot, :, pl.ds(pl.multiple_of(g * lanes, lanes), lanes)].astype(F32)
            cells[b, pl.ds(base + 2 * g, rows, stride=cell_pitch), :] = jnp.where(low_half, both, 0.0)
            other = jnp.where(low_half, pltpu.roll(both, edge, 1), 0.0)
            cells[b, pl.ds(base + 2 * g + 1, rows, stride=cell_pitch), :] = other
            return carry

        lax.fori_loop(0, per_chunk - (q == chunks - 1), one, 0, unroll=True)

    def spread(g, carry):
        for k in range(4):
            k0 = 4 * g + k
            at = pl.ds(pl.multiple_of(k0 * k1_count, k1_count), k1_count)
            k_rows[pl.ds(k0 * k_pitch, k1_count), :] = v_parts[0, at, :]
        return carry

    def send_own(u):
        if u >= chunks:
            x_comes[u - chunks].wait_recv()
        z_boxes[u].start()
        pl.when(side == 1)(y_here[u].start)
        by_core[0][u].start()
        if u >= chunks:
            unpack(u, 0, core)

    def pass_on(u):
        z_boxes[u].wait_recv()
        pl.when(side == 0)(y_pass[u].start)
        by_core[1][u].start()

    def pass_last(u):
        y_here[u].wait_recv()
        by_core[2][u].start()

    def pick(u):
        for g in range(3):
            by_core[g][u].wait_recv()
        for n in range(2):
            unpack(u, 1 + n, slots[n])

    for copy in x_sends:
        copy.start()
    stages = [(send_own, 0), (pass_on, chunks), (pass_last, chunks + 1), (pick, chunks + 2)]
    for step in range(units + chunks + 2):
        if step == chunks:
            clear_all()
            for u in range(chunks):
                unpack(u, 0, core)
        for stage, lag in stages:
            if 0 <= step - lag < units:
                stage(step - lag)
        if step == chunks + 1:
            for load in loads:
                load.wait()
            lax.fori_loop(0, edge // 2, spread, 0, unroll=2)

    corner_lane = lax.broadcasted_iota(jnp.int32, (1, lanes), 1)

    def corner(n):
        came = held[chunks - 1][slots[n], :, pl.ds(corner_at, lanes)].astype(F32)[0:1]
        return [jnp.sum(jnp.where(corner_lane == c, came, 0.0)).astype(jnp.int32) for c in range(3)]

    corners = [corner(n) for n in range(2)]
    shifts = [[jnp.clip(corners[n][c] - offsets_ref[0, c], -half, half) for c in range(3)] for n in range(2)]

    row = lax.broadcasted_iota(jnp.int32, (edge, lanes), 0)
    box_lane = lax.broadcasted_iota(jnp.int32, (edge, lanes), 1)

    e1_grid = e1_ref[slab]
    e2_grid = e2_ref[...]
    sel_lane = lax.broadcasted_iota(jnp.int32, (grid_len, lanes), 1)
    sel_row = lax.broadcasted_iota(jnp.int32, (grid_len, lanes), 0)

    def windows(d1, d2):
        pick_rows = (row + half + d1 == box_lane).astype(F32).astype(BF16)
        top = dot(pick_rows, e1_grid[:grid_len]).astype(BF16)
        bottom = dot(pick_rows, e1_grid[grid_len:]).astype(BF16)
        pick_cols = ((sel_lane + half + d2 == sel_row) & (sel_lane < edge)).astype(F32).astype(BF16)
        return jnp.concatenate([top, bottom], 0), dot(e2_grid, pick_cols).astype(BF16)

    e1_own[...], e2_own[...] = windows(0, 0)
    for n in range(2):
        e1_far[n], e2_far[n] = windows(shifts[n][1], shifts[n][2])

    def moved(b, c0, d0, d1, d2):
        source = c0 + d0
        at = jnp.where((source >= 0) & (source < edge), source, edge)
        block = cells[b, pl.ds(at * cell_pitch + half + d1, edge), :]
        return pltpu.roll(block, (-d2) & (lanes - 1), 1)

    batch = 4

    def forward(step, carry):
        z = []
        for j in range(batch):
            c0 = step * batch + j
            own = cells[0, pl.ds(c0 * cell_pitch + half, edge), :]
            for n in range(2):
                d0, d1, d2 = shifts[n]
                partner = moved(1 + n, c0, -d0, -d1, -d2)
                here[n, pl.ds(pl.multiple_of(c0 * edge, edge), edge), :] = partner
                z.append((own * partner).astype(BF16))
        z = dot(jnp.concatenate(z, 0), jnp.concatenate([f2_ref[0], f2_ref[1]], 1)).astype(BF16)
        for j in range(batch):
            c0 = step * batch + j
            mine = [z[(2 * j + n) * edge : (2 * j + n + 1) * edge] for n in range(2)]
            mine = jnp.concatenate(
                [jnp.concatenate([m[:, :grid_len], m[:, grid_len:]], 0) for m in mine], 1
            )
            y = dot(f1_ref[slab], mine)
            for n in range(2):
                part = y[:, n * grid_len : (n + 1) * grid_len]
                y_parts[n, pl.ds(c0, k1_count, stride=y_pitch), :] = part[:k1_count]
                y_parts[n, pl.ds(edge + c0, k1_count, stride=y_pitch), :] = part[k1_count:]
        return carry

    lax.fori_loop(0, edge // batch, forward, 0, unroll=4)

    def middle(k1, carry):
        at = pl.ds(k1 * y_pitch, 2 * edge)
        y = jnp.concatenate([y_parts[n, at, :].astype(BF16) for n in range(2)], 1)
        x = dot(f0_ref[...], y)
        k = k_rows[pl.ds(k1, grid_len, stride=k_pitch), :]
        k = jnp.concatenate([k, k], 1)
        w = jnp.concatenate([(x[:grid_len] * k).astype(BF16), (x[grid_len:] * k).astype(BF16)], 0)
        v = dot(jnp.concatenate([e0_ref[0], e0_ref[1]], 1), w)
        for n in range(2):
            part = v[:, n * grid_len : (n + 1) * grid_len]
            v_parts[n, pl.ds(k1, grid_len, stride=v_pitch), :] = part[:grid_len]
            v_parts[n, pl.ds(k1_count + k1, grid_len, stride=v_pitch), :] = part[grid_len:]
        return carry

    lax.fori_loop(0, k1_count, middle, 0, unroll=8)

    def v_rows(n, u0):
        u0 = jnp.clip(u0, 0, grid_len - 1)
        return v_parts[n, pl.ds(u0 * v_pitch, 2 * k1_count), :].astype(BF16)

    piece = own_terms.shape[1]
    pieces = rows // piece
    numbers = slab_count * pieces
    away = numbers - pieces

    parts = 4
    part_width = edge * edge // parts
    cols = [pl.ds(h * part_width, part_width) for h in range(parts)]

    def over_core(t, h):
        return remote(
            to_core.at[t, :, :, cols[h]], from_core.at[t, :, :, cols[h]], core_send.at[t, h], core_recv.at[t, h], sibling, slab
        )

    def over_y(t, h):
        return remote(to_y.at[t, :, cols[h]], from_y.at[t, :, cols[h]], y_send.at[t, h], y_recv.at[t, h], across, slab)

    def over_z(t, h):
        return remote(to_z.at[t, :, cols[h]], from_z.at[t, :, cols[h]], z_send.at[t, h], z_recv.at[t, h], ahead, slab)

    def over_x(t):
        target = lax.rem(slab + 1 + t // pieces, slab_count)
        return remote(to_x.at[t], from_x.at[t], x_send.at[t], x_recv.at[t], i, target)

    def first_row(number):
        return lax.rem(slab + 1 + number // pieces, slab_count) * rows + lax.rem(number, pieces) * piece

    def merged(b, g):
        lo = terms[b, pl.ds(2 * g, piece, stride=term_pitch), :]
        hi = terms[b, pl.ds(2 * g + 1, piece, stride=term_pitch), :]
        return lo + pltpu.roll(hi, edge, 1)

    def compute_far(number):
        first = first_row(number)

        def backward(step, inner):
            for n in range(2):
                d0, d1, d2 = shifts[n]
                u = []
                for j in range(0, batch, 2):
                    u0 = half + d0 + first + step * batch + j
                    v = jnp.concatenate([v_rows(n, u0), v_rows(n, u0 + 1)], 1)
                    part = dot(e1_far[n], v).astype(BF16)
                    for c in range(2):
                        mine = part[:, c * grid_len : (c + 1) * grid_len]
                        u.append(jnp.concatenate([mine[:edge], mine[edge:]], 1))
                field = dot(jnp.concatenate(u, 0), e2_far[n])
                for j in range(batch):
                    there = moved(0, first + step * batch + j, d0, d1, d2)
                    to = pl.ds((step * batch + j) * term_pitch, edge)
                    terms[1 + n, to, :] = field[j * edge : (j + 1) * edge] * there
            return inner

        lax.fori_loop(0, piece // batch, backward, 0, unroll=True)

        def pack(g, inner):
            at = pl.ds(pl.multiple_of(g * lanes, lanes), lanes)
            both = [merged(1 + n, g) for n in range(2)]

            def share(slot):
                return jnp.where(slots[0] == slot, both[0], jnp.where(slots[1] == slot, both[1], 0.0))

            for group in range(3):
                to_core[number, group, :, at] = share(2 * group + 1 - core).astype(BF16)
            for group in range(1, 3):
                kept[number, group - 1, :, at] = share(2 * group + core)
            own_terms[number, :, at] = jnp.zeros((piece, lanes), F32)
            return inner

        for h in range(parts):
            share_of = edge // 2 // parts
            lax.fori_loop(h * share_of, (h + 1) * share_of, pack, 0, unroll=True)
            over_core(number, h).start()

    def compute_own(number):
        first = first_row(number)

        def backward(step, inner):
            u = []
            for j in range(batch):
                c0 = first + step * batch + j
                v = jnp.concatenate([v_rows(n, half + c0) for n in range(2)], 1)
                part = dot(e1_own[...], v).astype(BF16)
                for n in range(2):
                    mine = part[:, n * grid_len : (n + 1) * grid_len]
                    u.append(jnp.concatenate([mine[:edge], mine[edge:]], 1))
            field = dot(jnp.concatenate(u, 0), e2_own[...])
            for j in range(batch):
                c0 = first + step * batch + j
                at = pl.ds(pl.multiple_of(c0 * edge, edge), edge)
                own = field[2 * j * edge : (2 * j + 1) * edge] * here[0, at, :]
                own += field[(2 * j + 1) * edge : (2 * j + 2) * edge] * here[1, at, :]
                terms[0, pl.ds((step * batch + j) * term_pitch, edge), :] = own
            return inner

        lax.fori_loop(0, piece // batch, backward, 0, unroll=True)

        def pack(g, inner):
            own_terms[number, :, pl.ds(pl.multiple_of(g * lanes, lanes), lanes)] += merged(0, g)
            return inner

        lax.fori_loop(0, edge // 2, pack, 0, unroll=8)

    def after_core(t):
        for h in range(parts):
            over_core(t, h).wait_recv()
            at = cols[h]
            to_y[t, :, at] = (kept[t, 1, :, at] + from_core[t, 2, :, at].astype(F32)).astype(BF16)
            over_y(t, h).start()
            own_terms[t, :, at] += from_core[t, 0, :, at].astype(F32)
            kept[t, 0, :, at] += from_core[t, 1, :, at].astype(F32)

    def after_y(t):
        for h in range(parts):
            over_y(t, h).wait_recv()
            at = cols[h]
            came = from_y[t, :, at].astype(F32)
            to_z[t, :, at] = (kept[t, 0, :, at] + jnp.where(side == 0, came, 0.0)).astype(BF16)
            over_z(t, h).start()
            own_terms[t, :, at] += jnp.where(side == 1, came, 0.0)

    def after_z(t):
        for h in range(parts):
            over_z(t, h).wait_recv()
            own_terms[t, :, cols[h]] += from_z[t, :, cols[h]].astype(F32)

        @pl.when(t < away)
        def _():
            to_x[t] = own_terms[t].astype(BF16)
            over_x(t).start()

    def one_step(step, carry):
        for stage, lag in ((after_core, 1), (after_y, 2), (after_z, 3), (compute_far, 0)):
            pl.when((step >= lag) & (step < numbers + lag))(functools.partial(stage, step - lag))
        late = step >= away + 2
        pl.when((step < away) | (late & (step < numbers + 2)))(
            functools.partial(compute_own, jnp.where(late, step - 2, step))
        )
        return carry

    lax.fori_loop(0, numbers + 3, one_step, 0)

    for q in range(pieces):
        total = own_terms[away + q]
        for k in range(slab_count - 1):
            over_x(k * pieces + q).wait_recv()
            total += from_x[k * pieces + q].astype(F32)
        out_ref[pl.ds(q * piece, piece), :] = total
    for t in range(numbers):
        for h in range(parts):
            over_core(t, h).wait_send()
            over_y(t, h).wait_send()
            over_z(t, h).wait_send()
        if t < away:
            over_x(t).wait_send()
    for copy in x_sends + z_boxes + y_here + by_core[0] + by_core[1] + by_core[2]:
        copy.wait_send()


def pair_terms(orbitals, partners, offsets, kernel):
    orb_count = lax.axis_size("orb")
    slab_count = lax.axis_size("slab")
    rows, cells = orbitals.shape[1:]
    box_edge = slab_count * rows
    grid_len, k1_count = kernel.shape[0], kernel.shape[1]
    tables = make_tables(box_edge, slab_count)
    smem = pl.BlockSpec(memory_space=pltpu.SMEM)
    vmem = pl.BlockSpec(memory_space=pltpu.VMEM)
    chunks = 3 if (cells // 128 + 1) % 3 == 0 else 1
    units = slab_count * chunks
    cell_rows = (box_edge + 1) * (box_edge + box_edge // 2 + 1) + box_edge // 2 - 1
    arrays = [kernel.reshape(grid_len * k1_count, grid_len)] + tables
    lanes = 2 * box_edge
    piece = min(rows, 16)
    pieces = rows // piece
    numbers = slab_count * pieces
    sent = numbers - pieces
    flat = (piece, cells)
    dma = pltpu.SemaphoreType.DMA
    return pl.pallas_call(
        functools.partial(pair_kernel, orb_count, slab_count, box_edge, k1_count, chunks),
        out_shape=jax.ShapeDtypeStruct((rows, cells), F32),
        in_specs=[smem, smem, vmem] + [pl.BlockSpec(memory_space=pl.ANY)] * 7,
        out_specs=vmem,
        scratch_shapes=[pltpu.VMEM(a.shape, a.dtype) for a in tables] + [
            dma((len(arrays),)),
            dma((slab_count, chunks)), dma((slab_count, chunks)), dma((units,)), dma((units,)), dma((units,)), dma((units,)),
            dma((3, units)), dma((3, units)),
            pltpu.VMEM((3, cell_rows, lanes), F32),
            pltpu.VMEM((2, cells, lanes), F32),
            pltpu.VMEM((2, k1_count * (2 * box_edge + 1), grid_len), F32),
            pltpu.VMEM((2, grid_len * (2 * k1_count + 1), grid_len), F32),
            pltpu.VMEM((grid_len * (k1_count + 1), grid_len), F32),
            pltpu.VMEM((3, piece * (box_edge + 1), lanes), F32),
            pltpu.VMEM((2 * box_edge, 2 * k1_count), BF16),
            pltpu.VMEM((2, 2 * box_edge, 2 * k1_count), BF16),
            pltpu.VMEM((2 * grid_len, lanes), BF16),
            pltpu.VMEM((2, 2 * grid_len, lanes), BF16),
        ] + [dma((sent,))] * 2 + [dma((numbers, 4))] * 6 + [
            pltpu.VMEM((numbers,) + flat, F32),
            pltpu.VMEM((numbers, 2) + flat, F32),
            pltpu.VMEM((numbers, 3) + flat, BF16),
            pltpu.VMEM((numbers, 3) + flat, BF16),
        ] + [pltpu.VMEM((numbers,) + flat, BF16)] * 4 + [pltpu.VMEM((sent,) + flat, BF16)] * 2 + [
            pltpu.VMEM((6, rows, (cells + lanes) // chunks), BF16)
        ] * units,
        compiler_params=pltpu.CompilerParams(
            collective_id=0, has_side_effects=True, vmem_limit_bytes=60 * 1024 * 1024
        ),
        name="pair_terms",
    )(partners, offsets, orbitals.reshape(rows, cells), *arrays)


def per_device(orbitals, partners, offsets, kernel):
    return pair_terms(orbitals, partners, offsets, kernel)[None]


def solution(mesh):
    return jax.shard_map(
        per_device,
        mesh=mesh,
        in_specs=(P("orb", "slab", None), P("orb", None), P("orb", None), P(None, "slab", None)),
        out_specs=P("orb", "slab", None),
        check_vma=False,
    )
```

```python
import functools
import math

import jax
import jax.numpy as jnp
import ml_dtypes
import numpy as np
from jax import lax
from jax.experimental import pallas as pl
from jax.experimental.pallas import tpu as pltpu
from jax.sharding import PartitionSpec as P

REACH = 4
F32 = jnp.float32
BF16 = jnp.bfloat16


def phases(places, frequency, grid_len, signed):
    wrapped = (places[:, None] * frequency[None, :]) % grid_len
    angles = wrapped.astype(np.float64) * (2.0 * math.pi / grid_len)
    return np.cos(angles), signed * np.sin(angles)


def block_form(cos, sin):
    return np.block([[cos, -sin], [sin, cos]])


def halves(table):
    return np.stack(np.split(table, 2, axis=1))


def make_tables(box_edge, slab_count):
    grid_len = 2 * box_edge
    half = box_edge // 2
    k1_count = grid_len // slab_count
    box = np.arange(box_edge) + half
    grid = np.arange(grid_len)
    cos, sin = phases(box, grid, grid_len, -1.0)
    f2 = np.zeros((2 * box_edge, 2 * grid_len))
    f2[:box_edge] = np.concatenate([cos, sin], 1)
    f0 = block_form(cos.T, sin.T)
    f1 = []
    e1 = []
    gcos, gsin = phases(grid, grid, grid_len, 1.0)
    for s in range(slab_count):
        mine = slice(s * k1_count, (s + 1) * k1_count)
        f1.append(block_form(cos.T[mine], sin.T[mine]))
        e1.append(block_form(gcos[:, mine], gsin[:, mine]))
    e0 = block_form(gcos, gsin)
    e2 = np.concatenate([gcos.T, -gsin.T], 0) / grid_len**3
    tables = [halves(f2), np.stack(f1), f0, halves(e0), np.stack(e1), e2]
    return [t.astype(np.float32).astype(ml_dtypes.bfloat16) for t in tables]


def dot(a, b):
    return jnp.dot(a, b, preferred_element_type=F32)


def neighbours(orb_count):
    i = lax.axis_index("orb")
    core, side = lax.rem(i, 2), lax.rem(i // 2, 2)
    sibling = i + 1 - 2 * core
    across = i + 2 - 4 * side
    behind = lax.rem(i + orb_count - REACH, orb_count)
    ahead = lax.rem(i + REACH, orb_count)
    return i, core, side, sibling, across, behind, ahead


def slot_of(partner, i, side, orb_count):
    hop = jnp.minimum(lax.rem(partner - i + orb_count, orb_count), REACH)
    target = lax.rem(i, REACH) + hop
    group, place = target // REACH, lax.rem(target, REACH)
    return 2 * jnp.where(place // 2 == side, group, 2) + lax.rem(place, 2)


def remote(src, dst, send_sem, recv_sem, orb, slab):
    return pltpu.make_async_remote_copy(
        src_ref=src, dst_ref=dst, send_sem=send_sem, recv_sem=recv_sem,
        device_id=(orb, slab), device_id_type=pl.DeviceIdType.MESH,
    )


def greet(peers):
    barrier = pltpu.get_barrier_semaphore()
    for peer in peers:
        pl.semaphore_signal(barrier, inc=1, device_id=peer, device_id_type=pl.DeviceIdType.MESH)
    pl.semaphore_wait(barrier, len(peers))


def pair_kernel(
    orb_count, slab_count, box_edge, k1_count, chunks,
    partners_ref, offsets_ref, orbital_ref, kernel_in, f2_in, f1_in, f0_in, e0_in, e1_in, e2_in,
    out_ref,
    f2_ref, f1_ref, f0_ref, e0_ref, e1_ref, e2_ref, in_sem,
    own_send, own_recv, ahead_send, ahead_recv, side_send, side_recv, sib_send, sib_recv,
    cells, here, y_parts, v_parts, k_rows, terms, e1_own, e1_far, e2_own, e2_far,
    x_send, x_recv, core_send, core_recv, y_send, y_recv, z_send, z_recv,
    own_terms, kept, to_core, from_core, to_y, from_y, to_z, from_z, to_x, from_x,
    *held,
):
    edge = box_edge
    grid_len = 2 * edge
    half = edge // 2
    lanes = 2 * edge
    rows, cell_count = orbital_ref.shape
    i, core, side, sibling, across, behind, ahead = neighbours(orb_count)
    slab = lax.axis_index("slab")
    others = [lax.rem(slab + k, slab_count) for k in range(slab_count)]
    kernel_ref = v_parts.at[0, pl.ds(0, grid_len * k1_count), :]
    arrays_in = [kernel_in, f2_in, f1_in, f0_in, e0_in, e1_in, e2_in]
    arrays = [kernel_ref, f2_ref, f1_ref, f0_ref, e0_ref, e1_ref, e2_ref]
    loads = [pltpu.make_async_copy(a, b, in_sem.at[k]) for k, (a, b) in enumerate(zip(arrays_in, arrays))]
    for k in (6, 5, 1, 2, 0, 3, 4):
        loads[k].start()

    per_chunk = (cell_count + lanes) // (lanes * chunks)
    width = per_chunk * lanes
    units = slab_count * chunks
    corner_at = (per_chunk - 1) * lanes
    lane = lax.broadcasted_iota(jnp.int32, (rows, lanes), 1)
    low_half = lane < edge
    own_corner = jnp.zeros((rows, lanes), F32)
    for c in range(3):
        own_corner = jnp.where(lane == c, offsets_ref[0, c].astype(F32), own_corner)
    for q in range(chunks):
        size = width if q < chunks - 1 else width - lanes
        held[q][core, :, pl.ds(0, size)] = orbital_ref[:, pl.ds(q * width, size)]
    held[chunks - 1][core, :, pl.ds(corner_at, lanes)] = own_corner.astype(BF16)
    greet([(p, slab) for p in (sibling, across, behind, ahead)] + [(i, o) for o in others[1:]])

    def along(u, source, target, send, recv, to):
        return remote(held[u].at[source], held[u].at[target], send, recv, to, slab)

    def to_slab(k, q):
        back = slab_count - k
        return remote(held[q].at[core], held[back * chunks + q].at[core], own_send.at[k, q], own_recv.at[k, q], i, others[k])

    def from_slab(k, q):
        back = slab_count - k
        return remote(held[q].at[core], held[k * chunks + q].at[core], own_send.at[back, q], own_recv.at[back, q], i, others[k])

    x_sends = [to_slab(k, q) for k in range(1, slab_count) for q in range(chunks)]
    x_comes = [from_slab(k, q) for k in range(1, slab_count) for q in range(chunks)]
    z_boxes = [along(u, core, 2 + core, ahead_send.at[u], ahead_recv.at[u], behind) for u in range(units)]
    y_here = [along(u, core, 4 + core, side_send.at[u], side_recv.at[u], across) for u in range(units)]
    y_pass = [along(u, 2 + core, 4 + core, side_send.at[u], side_recv.at[u], across) for u in range(units)]
    by_core = [
        [along(u, 2 * g + core, 2 * g + core, sib_send.at[g, u], sib_recv.at[g, u], sibling) for u in range(units)]
        for g in range(3)
    ]
    slots = [slot_of(partners_ref[0, n], i, side, orb_count) for n in range(2)]
    cell_pitch = edge + half + 1
    term_pitch = edge + 1
    y_pitch = 2 * edge + 1
    v_pitch = 2 * k1_count + 1
    k_pitch = k1_count + 1

    no_rows = jnp.zeros((half + 8, lanes), F32)

    def clear(c0, carry):
        for b in range(3):
            cells[b, pl.ds(c0 * cell_pitch + cell_pitch - 1, half + 8), :] = no_rows
        return carry

    def clear_all():
        for b in range(3):
            cells[b, pl.ds(0, half), :] = jnp.zeros((half, lanes), F32)
        lax.fori_loop(0, edge, clear, 0, unroll=4)
        for b in range(3):
            cells[b, pl.ds(edge * cell_pitch, edge + 2 * half), :] = jnp.zeros((edge + 2 * half, lanes), F32)

    def unpack(u, b, slot):
        k, q = u // chunks, u % chunks
        base = others[k] * (rows * cell_pitch) + half + 2 * q * per_chunk

        def one(g, carry):
            both = held[u][slot, :, pl.ds(pl.multiple_of(g * lanes, lanes), lanes)].astype(F32)
            cells[b, pl.ds(base + 2 * g, rows, stride=cell_pitch), :] = jnp.where(low_half, both, 0.0)
            other = jnp.where(low_half, pltpu.roll(both, edge, 1), 0.0)
            cells[b, pl.ds(base + 2 * g + 1, rows, stride=cell_pitch), :] = other
            return carry

        lax.fori_loop(0, per_chunk - (q == chunks - 1), one, 0, unroll=True)

    def spread(g, carry):
        for k in range(4):
            k0 = 4 * g + k
            at = pl.ds(pl.multiple_of(k0 * k1_count, k1_count), k1_count)
            k_rows[pl.ds(k0 * k_pitch, k1_count), :] = v_parts[0, at, :]
        return carry

    def send_own(u):
        if u >= chunks:
            x_comes[u - chunks].wait_recv()
        z_boxes[u].start()
        pl.when(side == 1)(y_here[u].start)
        by_core[0][u].start()
        if u >= chunks:
            unpack(u, 0, core)

    def pass_on(u):
        z_boxes[u].wait_recv()
        pl.when(side == 0)(y_pass[u].start)
        by_core[1][u].start()

    def pass_last(u):
        y_here[u].wait_recv()
        by_core[2][u].start()

    def pick(u):
        for g in range(3):
            by_core[g][u].wait_recv()
        for n in range(2):
            unpack(u, 1 + n, slots[n])

    for copy in x_sends:
        copy.start()
    stages = [(send_own, 0), (pass_on, chunks), (pass_last, chunks + 1), (pick, chunks + 2)]
    for step in range(units + chunks + 2):
        if step == chunks:
            clear_all()
            for u in range(chunks):
                unpack(u, 0, core)
        for stage, lag in stages:
            if 0 <= step - lag < units:
                stage(step - lag)
        if step == chunks + 1:
            for load in loads:
                load.wait()
            lax.fori_loop(0, edge // 2, spread, 0, unroll=2)

    corner_lane = lax.broadcasted_iota(jnp.int32, (1, lanes), 1)

    def corner(n):
        came = held[chunks - 1][slots[n], :, pl.ds(corner_at, lanes)].astype(F32)[0:1]
        return [jnp.sum(jnp.where(corner_lane == c, came, 0.0)).astype(jnp.int32) for c in range(3)]

    corners = [corner(n) for n in range(2)]
    shifts = [[jnp.clip(corners[n][c] - offsets_ref[0, c], -half, half) for c in range(3)] for n in range(2)]

    row = lax.broadcasted_iota(jnp.int32, (edge, lanes), 0)
    box_lane = lax.broadcasted_iota(jnp.int32, (edge, lanes), 1)

    e1_grid = e1_ref[slab]
    e2_grid = e2_ref[...]
    sel_lane = lax.broadcasted_iota(jnp.int32, (grid_len, lanes), 1)
    sel_row = lax.broadcasted_iota(jnp.int32, (grid_len, lanes), 0)

    def windows(d1, d2):
        pick_rows = (row + half + d1 == box_lane).astype(F32).astype(BF16)
        top = dot(pick_rows, e1_grid[:grid_len]).astype(BF16)
        bottom = dot(pick_rows, e1_grid[grid_len:]).astype(BF16)
        pick_cols = ((sel_lane + half + d2 == sel_row) & (sel_lane < edge)).astype(F32).astype(BF16)
        return jnp.concatenate([top, bottom], 0), dot(e2_grid, pick_cols).astype(BF16)

    e1_own[...], e2_own[...] = windows(0, 0)
    for n in range(2):
        e1_far[n], e2_far[n] = windows(shifts[n][1], shifts[n][2])

    def moved(b, c0, d0, d1, d2):
        source = c0 + d0
        at = jnp.where((source >= 0) & (source < edge), source, edge)
        block = cells[b, pl.ds(at * cell_pitch + half + d1, edge), :]
        return pltpu.roll(block, (-d2) & (lanes - 1), 1)

    batch = 8

    def forward(step, carry):
        z = []
        for j in range(batch):
            c0 = step * batch + j
            own = cells[0, pl.ds(c0 * cell_pitch + half, edge), :]
            for n in range(2):
                d0, d1, d2 = shifts[n]
                partner = moved(1 + n, c0, -d0, -d1, -d2)
                here[n, pl.ds(pl.multiple_of(c0 * edge, edge), edge), :] = partner
                z.append((own * partner).astype(BF16))
        z = dot(jnp.concatenate(z, 0), jnp.concatenate([f2_ref[0], f2_ref[1]], 1)).astype(BF16)
        for j in range(batch):
            c0 = step * batch + j
            mine = [z[(2 * j + n) * edge : (2 * j + n + 1) * edge] for n in range(2)]
            mine = jnp.concatenate(
                [jnp.concatenate([m[:, :grid_len], m[:, grid_len:]], 0) for m in mine], 1
            )
            y = dot(f1_ref[slab], mine)
            for n in range(2):
                part = y[:, n * grid_len : (n + 1) * grid_len]
                y_parts[n, pl.ds(c0, k1_count, stride=y_pitch), :] = part[:k1_count]
                y_parts[n, pl.ds(edge + c0, k1_count, stride=y_pitch), :] = part[k1_count:]
        return carry

    lax.fori_loop(0, edge // batch, forward, 0, unroll=2)

    def middle(k1, carry):
        at = pl.ds(k1 * y_pitch, 2 * edge)
        y = jnp.concatenate([y_parts[n, at, :].astype(BF16) for n in range(2)], 1)
        x = dot(f0_ref[...], y)
        k = k_rows[pl.ds(k1, grid_len, stride=k_pitch), :]
        k = jnp.concatenate([k, k], 1)
        w = jnp.concatenate([(x[:grid_len] * k).astype(BF16), (x[grid_len:] * k).astype(BF16)], 0)
        v = dot(jnp.concatenate([e0_ref[0], e0_ref[1]], 1), w)
        for n in range(2):
            part = v[:, n * grid_len : (n + 1) * grid_len]
            v_parts[n, pl.ds(k1, grid_len, stride=v_pitch), :] = part[:grid_len]
            v_parts[n, pl.ds(k1_count + k1, grid_len, stride=v_pitch), :] = part[grid_len:]
        return carry

    lax.fori_loop(0, k1_count, middle, 0, unroll=8)

    def v_rows(n, u0):
        u0 = jnp.clip(u0, 0, grid_len - 1)
        return v_parts[n, pl.ds(u0 * v_pitch, 2 * k1_count), :].astype(BF16)

    piece = own_terms.shape[1]
    pieces = rows // piece
    numbers = slab_count * pieces
    away = numbers - pieces

    parts = 4
    part_width = edge * edge // parts
    cols = [pl.ds(h * part_width, part_width) for h in range(parts)]

    def over_core(t, h):
        return remote(
            to_core.at[t, :, :, cols[h]], from_core.at[t, :, :, cols[h]], core_send.at[t, h], core_recv.at[t, h], sibling, slab
        )

    def over_y(t, h):
        return remote(to_y.at[t, :, cols[h]], from_y.at[t, :, cols[h]], y_send.at[t, h], y_recv.at[t, h], across, slab)

    def over_z(t, h):
        return remote(to_z.at[t, :, cols[h]], from_z.at[t, :, cols[h]], z_send.at[t, h], z_recv.at[t, h], ahead, slab)

    def over_x(t):
        target = lax.rem(slab + 1 + t // pieces, slab_count)
        return remote(to_x.at[t], from_x.at[t], x_send.at[t], x_recv.at[t], i, target)

    def first_row(number):
        return lax.rem(slab + 1 + number // pieces, slab_count) * rows + lax.rem(number, pieces) * piece

    def merged(b, g):
        lo = terms[b, pl.ds(2 * g, piece, stride=term_pitch), :]
        hi = terms[b, pl.ds(2 * g + 1, piece, stride=term_pitch), :]
        return lo + pltpu.roll(hi, edge, 1)

    def compute_far(number):
        first = first_row(number)

        def backward(step, inner):
            for n in range(2):
                d0, d1, d2 = shifts[n]
                u = []
                for j in range(0, batch, 2):
                    u0 = half + d0 + first + step * batch + j
                    v = jnp.concatenate([v_rows(n, u0), v_rows(n, u0 + 1)], 1)
                    part = dot(e1_far[n], v).astype(BF16)
                    for c in range(2):
                        mine = part[:, c * grid_len : (c + 1) * grid_len]
                        u.append(jnp.concatenate([mine[:edge], mine[edge:]], 1))
                field = dot(jnp.concatenate(u, 0), e2_far[n])
                for j in range(batch):
                    there = moved(0, first + step * batch + j, d0, d1, d2)
                    to = pl.ds((step * batch + j) * term_pitch, edge)
                    terms[1 + n, to, :] = field[j * edge : (j + 1) * edge] * there
            return inner

        lax.fori_loop(0, piece // batch, backward, 0, unroll=True)

        def pack(g, inner):
            at = pl.ds(pl.multiple_of(g * lanes, lanes), lanes)
            both = [merged(1 + n, g) for n in range(2)]

            def share(slot):
                return jnp.where(slots[0] == slot, both[0], jnp.where(slots[1] == slot, both[1], 0.0))

            for group in range(3):
                to_core[number, group, :, at] = share(2 * group + 1 - core).astype(BF16)
            for group in range(1, 3):
                kept[number, group - 1, :, at] = share(2 * group + core)
            own_terms[number, :, at] = jnp.zeros((piece, lanes), F32)
            return inner

        for h in range(parts):
            share_of = edge // 2 // parts
            lax.fori_loop(h * share_of, (h + 1) * share_of, pack, 0, unroll=True)
            over_core(number, h).start()

    def compute_own(number):
        first = first_row(number)

        def backward(step, inner):
            u = []
            for j in range(batch):
                c0 = first + step * batch + j
                v = jnp.concatenate([v_rows(n, half + c0) for n in range(2)], 1)
                part = dot(e1_own[...], v).astype(BF16)
                for n in range(2):
                    mine = part[:, n * grid_len : (n + 1) * grid_len]
                    u.append(jnp.concatenate([mine[:edge], mine[edge:]], 1))
            field = dot(jnp.concatenate(u, 0), e2_own[...])
            for j in range(batch):
                c0 = first + step * batch + j
                at = pl.ds(pl.multiple_of(c0 * edge, edge), edge)
                own = field[2 * j * edge : (2 * j + 1) * edge] * here[0, at, :]
                own += field[(2 * j + 1) * edge : (2 * j + 2) * edge] * here[1, at, :]
                terms[0, pl.ds((step * batch + j) * term_pitch, edge), :] = own
            return inner

        lax.fori_loop(0, piece // batch, backward, 0, unroll=True)

        def pack(g, inner):
            own_terms[number, :, pl.ds(pl.multiple_of(g * lanes, lanes), lanes)] += merged(0, g)
            return inner

        lax.fori_loop(0, edge // 2, pack, 0, unroll=8)

    def after_core(t):
        for h in range(parts):
            over_core(t, h).wait_recv()
            at = cols[h]
            to_y[t, :, at] = (kept[t, 1, :, at] + from_core[t, 2, :, at].astype(F32)).astype(BF16)
            over_y(t, h).start()
            own_terms[t, :, at] += from_core[t, 0, :, at].astype(F32)
            kept[t, 0, :, at] += from_core[t, 1, :, at].astype(F32)

    def after_y(t):
        for h in range(parts):
            over_y(t, h).wait_recv()
            at = cols[h]
            came = from_y[t, :, at].astype(F32)
            to_z[t, :, at] = (kept[t, 0, :, at] + jnp.where(side == 0, came, 0.0)).astype(BF16)
            over_z(t, h).start()
            own_terms[t, :, at] += jnp.where(side == 1, came, 0.0)

    def after_z(t):
        for h in range(parts):
            over_z(t, h).wait_recv()
            own_terms[t, :, cols[h]] += from_z[t, :, cols[h]].astype(F32)

        @pl.when(t < away)
        def _():
            to_x[t] = own_terms[t].astype(BF16)
            over_x(t).start()

    def one_step(step, carry):
        for stage, lag in ((after_core, 1), (after_y, 2), (after_z, 3), (compute_far, 0)):
            pl.when((step >= lag) & (step < numbers + lag))(functools.partial(stage, step - lag))
        late = step >= away + 2
        pl.when((step < away) | (late & (step < numbers + 2)))(
            functools.partial(compute_own, jnp.where(late, step - 2, step))
        )
        return carry

    lax.fori_loop(0, numbers + 3, one_step, 0)

    for q in range(pieces):
        total = own_terms[away + q]
        for k in range(slab_count - 1):
            over_x(k * pieces + q).wait_recv()
            total += from_x[k * pieces + q].astype(F32)
        out_ref[pl.ds(q * piece, piece), :] = total
    for t in range(numbers):
        for h in range(parts):
            over_core(t, h).wait_send()
            over_y(t, h).wait_send()
            over_z(t, h).wait_send()
        if t < away:
            over_x(t).wait_send()
    for copy in x_sends + z_boxes + y_here + by_core[0] + by_core[1] + by_core[2]:
        copy.wait_send()


def pair_terms(orbitals, partners, offsets, kernel):
    orb_count = lax.axis_size("orb")
    slab_count = lax.axis_size("slab")
    rows, cells = orbitals.shape[1:]
    box_edge = slab_count * rows
    grid_len, k1_count = kernel.shape[0], kernel.shape[1]
    tables = make_tables(box_edge, slab_count)
    smem = pl.BlockSpec(memory_space=pltpu.SMEM)
    vmem = pl.BlockSpec(memory_space=pltpu.VMEM)
    chunks = 3 if (cells // 128 + 1) % 3 == 0 else 1
    units = slab_count * chunks
    cell_rows = (box_edge + 1) * (box_edge + box_edge // 2 + 1) + box_edge // 2 - 1
    arrays = [kernel.reshape(grid_len * k1_count, grid_len)] + tables
    lanes = 2 * box_edge
    piece = min(rows, 16)
    pieces = rows // piece
    numbers = slab_count * pieces
    sent = numbers - pieces
    flat = (piece, cells)
    dma = pltpu.SemaphoreType.DMA
    return pl.pallas_call(
        functools.partial(pair_kernel, orb_count, slab_count, box_edge, k1_count, chunks),
        out_shape=jax.ShapeDtypeStruct((rows, cells), F32),
        in_specs=[smem, smem, vmem] + [pl.BlockSpec(memory_space=pl.ANY)] * 7,
        out_specs=vmem,
        scratch_shapes=[pltpu.VMEM(a.shape, a.dtype) for a in tables] + [
            dma((len(arrays),)),
            dma((slab_count, chunks)), dma((slab_count, chunks)), dma((units,)), dma((units,)), dma((units,)), dma((units,)),
            dma((3, units)), dma((3, units)),
            pltpu.VMEM((3, cell_rows, lanes), F32),
            pltpu.VMEM((2, cells, lanes), F32),
            pltpu.VMEM((2, k1_count * (2 * box_edge + 1), grid_len), F32),
            pltpu.VMEM((2, grid_len * (2 * k1_count + 1), grid_len), F32),
            pltpu.VMEM((grid_len * (k1_count + 1), grid_len), F32),
            pltpu.VMEM((3, piece * (box_edge + 1), lanes), F32),
            pltpu.VMEM((2 * box_edge, 2 * k1_count), BF16),
            pltpu.VMEM((2, 2 * box_edge, 2 * k1_count), BF16),
            pltpu.VMEM((2 * grid_len, lanes), BF16),
            pltpu.VMEM((2, 2 * grid_len, lanes), BF16),
        ] + [dma((sent,))] * 2 + [dma((numbers, 4))] * 6 + [
            pltpu.VMEM((numbers,) + flat, F32),
            pltpu.VMEM((numbers, 2) + flat, F32),
            pltpu.VMEM((numbers, 3) + flat, BF16),
            pltpu.VMEM((numbers, 3) + flat, BF16),
        ] + [pltpu.VMEM((numbers,) + flat, BF16)] * 4 + [pltpu.VMEM((sent,) + flat, BF16)] * 2 + [
            pltpu.VMEM((6, rows, (cells + lanes) // chunks), BF16)
        ] * units,
        compiler_params=pltpu.CompilerParams(
            collective_id=0, has_side_effects=True, vmem_limit_bytes=60 * 1024 * 1024
        ),
        name="pair_terms",
    )(partners, offsets, orbitals.reshape(rows, cells), *arrays)


def per_device(orbitals, partners, offsets, kernel):
    return pair_terms(orbitals, partners, offsets, kernel)[None]


def solution(mesh):
    return jax.shard_map(
        per_device,
        mesh=mesh,
        in_specs=(P("orb", "slab", None), P("orb", None), P("orb", None), P(None, "slab", None)),
        out_specs=P("orb", "slab", None),
        check_vma=False,
    )
```
